32 devices in a mesh: pole: 4 (over y, x), row: 2 (over core), col: 4 (over z).
Axes of the slice: x: 2, y: 2, z: 4, core: 2. Of those that a mesh axis runs over, the one named last changes fastest.
Arguments:
- inverse_tiles: float32 [8, 2, 2, 2048, 4096], P('pole', None, None, 'col', 'row'), may hold values from -6 to 6
- factor_block: float32 [8, 2, 4096, 512], P('pole', None, ('row', 'col')), may hold values from -0.09375 to 0.09375
- diag_inverse: float32 [8, 2, 2, 256, 256], P('pole'), may hold values from -6 to 6
- tile_pattern: int32 [8, 8], replicated, may hold values 0 or 1
- ancestor_blocks: int32 [2, 8], replicated, may hold values 0 or 1
- row_owner: int32 [4096, 1], P(('row', 'col')), may hold values from 0 to 3; in each aligned block of 512 rows (0 to 511, 512 to 1023, ...) at most 256 rows name the same one
- pole_weights: float32 [8, 2], replicated, may hold values from -4 to 4
- pole_order: int32 [8], replicated, may hold values from 0 to 7, each once
Outputs:
- inverse_rows: float32 [8, 2, 4096, 512], P('pole', None, ('row', 'col'))
- owned_density: float32 [4, 2048, 512], P('pole', ('row', 'col'))
- block_density: float32 [2, 256, 256], replicated
The draws below stay inside these ranges and needn't reach their ends.
Inputs may be any that keep to these rules, and one draw needn't show every extreme that they name: `row_owner`: in each aligned block of 512 rows (the rows of one device) no owner has more than 256 rows, and some owner has exactly 256 in some block.
All inputs are finite; a program needn't handle non-finite values.
Results may differ from the reference program's by a relative error of at most 0.000073.
Values sent between devices are 32-bit elements; how exact they have to be, the bound alone decides.
No kernel may reach another device: no remote copies, remote signals or barrier semaphores. Data moves between devices by JAX's collectives and lax.ppermute only.
A program may use at most 192 MiB of HBM per device.

```python
import math
import jax
import jax.numpy as jnp
import numpy as np
from jax import lax

S = 256
NSUP = 2
NA = 4096
POLES = 8
W = 512
NB = 8
BLK = 512
SEGR = 2048
CAP = 256
N_POLE = 4
N_ROW = 2


def plant(drawn, stream_key, low, high):
    place = [jax.random.randint(jax.random.fold_in(stream_key, axis), (), 0, length) for axis, length in enumerate(drawn.shape)]
    longest = drawn.shape.index(max(drawn.shape))
    neighbour = place[:longest] + [(place[longest] + 1) % drawn.shape[longest]] + place[longest + 1:]
    return drawn.at[tuple(place)].set(low).at[tuple(neighbour)].set(high)


def levels(key, extent, cuts, least, high):
    def one(axis_at, blocks):
        steps = jax.random.uniform(jax.random.fold_in(jax.random.fold_in(key, 6), axis_at), (blocks,), jnp.float32, least / len(cuts), high / len(cuts))
        return jnp.repeat(jnp.exp(steps), extent[axis_at] // blocks).reshape((-1,) + (1,) * (len(extent) - axis_at - 1))

    factor_of = one(*cuts[0])
    for cut in cuts[1:]:
        factor_of = factor_of * one(*cut)
    return factor_of


def shared_out(key, own, number, rows, amount, top, reach, lean):
    order = jax.random.permutation(key, amount)
    crowded, common = portions_of(amount, rows * top, reach, lean, True), portions_of(amount, rows * top, reach, lean, False)
    places = jnp.arange(amount)

    def named(sizes, rotation):
        used = int((sizes > 0).sum())
        fixed = max(1, used // 4)
        passed = fixed + (places - fixed + rotation * (used - fixed)) % max(1, amount - fixed)
        return jnp.zeros((amount,), jnp.int32).at[order[jnp.where(places < fixed, places, passed)]].set(jnp.asarray(sizes, jnp.int32))

    sizes = jnp.where(number % 4 == 0, named(crowded, number // 4), named(common, number - number // 4 - 1))
    mixed = jax.random.permutation(jax.random.fold_in(own, 3), amount)
    source_of, sink = mixed[0:amount // 2 * 2:2], mixed[1:amount // 2 * 2:2]
    room = jnp.minimum(sizes[source_of] - 1, reach - sizes[sink]) // 2
    room = jnp.where((source_of == order[0]) | (sink == order[0]) | (sizes[sink] == 0), 0, jnp.maximum(room, 0))
    passed = jax.random.randint(jax.random.fold_in(own, 4), (amount // 2,), 0, 1 << 20) % (room + 1)
    sizes = sizes.at[source_of].add(-passed).at[sink].add(passed)
    items = jnp.searchsorted(jnp.cumsum(sizes), jnp.arange(rows * top), side="right").astype(jnp.int32)
    grid = items.reshape(top, rows).T
    grid = grid[jax.random.permutation(jax.random.fold_in(own, 1), rows)]
    rotation = jax.random.randint(jax.random.fold_in(own, 2), (rows, 1), 0, top)
    return jnp.take_along_axis(grid, (jnp.arange(top)[None, :] + rotation) % top, axis=1)


def portions_of(amount, total, most, skew, full):
    loads = [(1 << 20) // math.isqrt(standing ** skew) + 1 for standing in range(1, amount + 1)]
    largest = most if full else min(most, max(-(-total // amount), total * loads[0] // sum(loads)))
    least = 1 if total - largest >= amount - 1 else 0
    counts, rest = [largest] + [least] * (amount - 1), total - largest - least * (amount - 1)
    while rest > 0:
        free = [i for i in range(1, amount) if counts[i] < largest] or [i for i in range(1, amount) if counts[i] < most]
        whole, budget = sum([loads[i] for i in free]), rest
        for i in free:
            addition = min(most - counts[i], max(1, budget * loads[i] // whole), rest)
            counts[i] = counts[i] + addition
            rest = rest - addition
    return np.array(counts)


def scatter_about(rng, dims, deviation, limit, cuts=(), kind=jnp.bfloat16):
    factor_of = levels(rng, dims, cuts, -0.22, 0.18) if cuts else 1.0
    values = jax.random.normal(rng, dims, jnp.float32) * deviation * factor_of
    return jnp.minimum(jnp.maximum(values, -limit), limit).astype(kind)


def setup_inputs(seed: int = 0) -> dict:
    key_list = jax.random.split(jax.random.key(seed), 9)
    inverse_tiles = scatter_about(key_list[0], (POLES, 2, N_ROW, SEGR, NA), 1.0, 6.0, ((0, 4), (3, 4), (4, 2)), jnp.float32)
    factor_block = scatter_about(key_list[1], (POLES, 2, NA, W), NA ** -0.5, 0.09375, ((0, 4), (2, 8)), jnp.float32)
    diag_inverse = scatter_about(key_list[2], (POLES, 2, NSUP, S, S), 1.0, 6.0, ((0, 4),), jnp.float32)
    tile_pattern = plant((jax.random.randint(key_list[3], (NB, NB), 0, 4) < 3).astype(jnp.int32), jax.random.fold_in(key_list[3], 1), 0, 1)
    ancestor_blocks = plant((jax.random.randint(key_list[4], (NSUP, NB), 0, 2) < 1).astype(jnp.int32), jax.random.fold_in(key_list[4], 1), 0, 1)
    row_owner_keys = jax.random.split(jax.random.fold_in(key_list[5], 1), NA // BLK)
    row_owner_turns = jax.random.permutation(jax.random.fold_in(key_list[5], 3), NA // BLK)
    row_owner = jax.vmap(lambda own, number: shared_out(jax.random.fold_in(key_list[5], 2), own, number, BLK, N_POLE, 1, CAP, 2))(row_owner_keys, row_owner_turns).reshape((NA, 1))
    pole_weights = scatter_about(key_list[6], (POLES, 2), 1.0, 4.0, (), jnp.float32)
    pole_order = jax.random.permutation(key_list[7], POLES).astype(jnp.int32)
    return {"inverse_tiles": inverse_tiles, "factor_block": factor_block, "diag_inverse": diag_inverse, "tile_pattern": tile_pattern, "ancestor_blocks": ancestor_blocks, "row_owner": row_owner, "pole_weights": pole_weights, "pole_order": pole_order}


def matmul_high(left, right):
    return jnp.dot(left, right, precision=lax.Precision.HIGHEST, preferred_element_type=jnp.float32)


def reference(inverse_tiles, factor_block, diag_inverse, tile_pattern, ancestor_blocks, row_owner, pole_weights, pole_order):
    tile_full = jnp.repeat(jnp.repeat(tile_pattern.astype(jnp.float32), BLK, axis=0), BLK, axis=1)
    keep_rows = jnp.repeat(jnp.repeat(ancestor_blocks.T.astype(jnp.float32), BLK, axis=0), S, axis=1)

    def pole_solve(packed):
        inv_part, fac_part, diag_part = packed
        matrix = inv_part.reshape(2, NA, NA) * tile_full
        factor = fac_part * keep_rows
        real_part = matmul_high(matrix[0], factor[0]) - matmul_high(matrix[1], factor[1])
        imag_part = matmul_high(matrix[0], factor[1]) + matmul_high(matrix[1], factor[0])
        rows_real = real_part * keep_rows
        rows_imag = imag_part * keep_rows
        fac_real = factor[0].reshape(NA, NSUP, S)
        fac_imag = factor[1].reshape(NA, NSUP, S)
        yr_split = rows_real.reshape(NA, NSUP, S)
        yi_split = rows_imag.reshape(NA, NSUP, S)

        def contract(first, second):
            return jnp.einsum("aks,akt->kst", first, second, precision=lax.Precision.HIGHEST)

        prod_real = contract(fac_real, yr_split) - contract(fac_imag, yi_split)
        prod_imag = contract(fac_real, yi_split) + contract(fac_imag, yr_split)
        green = jnp.stack([diag_part[0] - prod_real, diag_part[1] - prod_imag], axis=0)
        return jnp.stack([rows_real, rows_imag], axis=0), green

    inverse_rows, green_all = lax.map(pole_solve, (inverse_tiles, factor_block, diag_inverse))
    one_hot = (pole_order[:, None] == jnp.arange(POLES, dtype=jnp.int32)[None, :]).astype(jnp.float32)
    weights = matmul_high(one_hot, pole_weights)
    weight_real = weights[:, 0]
    weight_imag = weights[:, 1]
    block_density = jnp.sum(weight_real[:, None, None, None] * green_all[:, 1] + weight_imag[:, None, None, None] * green_all[:, 0], axis=0)
    density = jnp.sum(weight_real[:, None, None] * inverse_rows[:, 1] + weight_imag[:, None, None] * inverse_rows[:, 0], axis=0)
    owner_ids = row_owner[:, 0].reshape(NB, BLK)
    owner_hot = (owner_ids[:, :, None] == jnp.arange(N_POLE, dtype=jnp.int32)[None, None, :]).astype(jnp.int32)
    owner_rank = jnp.cumsum(owner_hot, axis=1) - owner_hot
    rank_own = jnp.sum(owner_hot * owner_rank, axis=2)
    slot_hit = (rank_own[:, :, None] == jnp.arange(CAP, dtype=jnp.int32)[None, None, :]).astype(jnp.float32)
    dens_blocks = density.reshape(NB, BLK, W)
    owned = jnp.einsum("btp,btc,btw->pbcw", owner_hot.astype(jnp.float32), slot_hit, dens_blocks, precision=lax.Precision.HIGHEST)
    owned_density = owned.reshape(N_POLE, NB * CAP, W)
    return inverse_rows, owned_density, block_density
```

```python
import functools

import jax
import jax.numpy as jnp
from jax import lax
from jax.experimental import pallas as pl
from jax.experimental.pallas import tpu as pltpu
from jax.sharding import PartitionSpec as P

BF16 = jnp.bfloat16
VMEM_BYTES = 48 * 1024 * 1024


def smem():
    return pl.BlockSpec(memory_space=pltpu.SMEM)


def anywhere():
    return pl.BlockSpec(memory_space=pl.ANY)


def halves(value):
    high = value.astype(BF16)
    return high, (value - high.astype(jnp.float32)).astype(BF16)


def lowest_of(mask):
    return mask & -mask


def piece_index(bit, pieces):
    index = jnp.int32(-1)
    for i in range(pieces):
        index = jnp.where(bit == (1 << i), i, index)
    return index


def plan_kernel(
    rows, cols, supers, steps, place, pattern, keep, factor,
    info, moves, tasks, pool, arrive_up, arrive_down, total, stage, load_sems, store_sems,
):
    row, col = place[0], place[1]
    width = factor.shape[3] // supers
    pieces = supers * cols
    loads = [
        pltpu.make_async_copy(
            factor.at[:, :, :, pl.ds(k * width, width)], stage.at[k], load_sems.at[k]
        )
        for k in range(supers)
    ]
    stores = [
        pltpu.make_async_copy(stage.at[k], pool.at[k * cols + col], store_sems.at[k])
        for k in range(supers)
    ]
    for load in loads:
        load.start()
    for load, store in zip(loads, stores):
        load.wait()
        store.start()
    source = [sum(1 << (k * cols + c) for k in range(supers)) for c in range(cols)]
    links = cols - 1

    def one_row(i, carry):
        r = lax.rem(row + 1 + i, rows)
        kept = jnp.int32(0)
        for k in range(supers):
            for c in range(cols):
                kept = kept | (keep[k, r * cols + c] << (k * cols + c))
        need = []
        for c2 in range(cols):
            mask = jnp.int32(0)
            for g in range(rows):
                bits = jnp.int32(0)
                for c in range(cols):
                    bits = bits | (pattern[g * cols + c2, r * cols + c] << c)
                for k in range(supers):
                    mask = mask | ((keep[k, g * cols + c2] * bits) << (k * cols))
            need.append(mask & kept & ~source[c2])
        up_need, down_need = [], []
        for l in range(links):
            above = functools.reduce(lambda a, b: a | b, need[l + 1 :])
            below = functools.reduce(lambda a, b: a | b, need[: l + 1])
            up_need.append(above & sum(source[: l + 1]))
            down_need.append(below & sum(source[l + 1 :]))

        def one_step(t, state):
            up_left, up_have, down_left, down_have, last = state
            up_bit, down_bit = [], []
            for l in range(links):
                ready = up_left[l] & up_have[l]
                pick = jnp.int32(0)
                for m in range(l, links):
                    part = ready & up_need[m]
                    pick = jnp.where(part != 0, part, pick)
                up_bit.append(lowest_of(pick))
                ready = down_left[l] & down_have[l + 1]
                pick = jnp.int32(0)
                for m in range(l, -1, -1):
                    part = ready & down_need[m]
                    pick = jnp.where(part != 0, part, pick)
                down_bit.append(lowest_of(pick))
            up_left = [left ^ bit for left, bit in zip(up_left, up_bit)]
            down_left = [left ^ bit for left, bit in zip(down_left, down_bit)]
            up_have = up_have[:1] + [have | bit for have, bit in zip(up_have[1:], up_bit)]
            down_have = [have | bit for have, bit in zip(down_have, down_bit)] + down_have[-1:]
            moved = functools.reduce(lambda a, b: a | b, up_bit + down_bit)
            last = jnp.where(moved != 0, t + 1, last)
            none = jnp.int32(0)
            send_up = sum([jnp.where(col == l, up_bit[l], none) for l in range(links)])
            send_down = sum([jnp.where(col == l + 1, down_bit[l], none) for l in range(links)])
            get_up = sum([jnp.where(col == l + 1, up_bit[l], none) for l in range(links)])
            get_down = sum([jnp.where(col == l, down_bit[l], none) for l in range(links)])
            for j, bit in enumerate((send_up, send_down, get_up, get_down)):
                moves[j, t] = piece_index(bit, pieces)
            return up_left, up_have, down_left, down_have, last

        own = [jnp.int32(s) for s in source]
        state = (up_need, own, down_need, own, jnp.int32(0))
        info[r] = lax.fori_loop(0, steps, one_step, state)[-1]
        return carry

    lax.fori_loop(0, rows, one_row, jnp.int32(0))
    for j in range(4):
        moves[j, steps] = -1

    shortest = info[row]
    for r in range(rows):
        shortest = jnp.minimum(shortest, info[r])
    ahead = jnp.int32(0)
    for r in range(rows):
        ahead = ahead | jnp.where((info[r] > info[row]) | ((info[r] == info[row]) & (r < row)), 1, 0)
    early = jnp.where(shortest > 0, ahead, 0)
    info[rows + 2 * supers] = early

    def one_compute(s, touched):
        line = jnp.where((s == 0) & (early != 0), steps + 1, s)
        before = jnp.maximum(s - 1, 0)
        items = []
        for j in range(2):
            own_item = jnp.where(keep[j, row * cols + col] != 0, j * cols + col, -1)
            items.append(jnp.where(s == 0, own_item, moves[2 + j, before]))
        count = jnp.int32(0)
        previous = jnp.int32(-1)
        for j in range(1 + 2 * rows):
            tasks[line, j] = 0
        for g in range(rows):
            relative = lax.rem(g - row + rows, rows)
            for item in items:
                safe = jnp.maximum(item, 0)
                k = safe // cols
                c = safe - k * cols
                live = (
                    (item >= 0)
                    & (keep[k, g * cols + col] != 0)
                    & (pattern[g * cols + col, row * cols + c] != 0)
                )
                target = g * supers + k
                seen = (touched >> target) & 1
                joined = jnp.where(previous == target, 1, 0)
                code = (
                    safe + g * 256 + relative * 4096 + (1 - seen) * 65536 + joined * 131072
                )

                @pl.when(live)
                def _():
                    tasks[line, 1 + count] = code

                previous = jnp.where(live, target, previous)
                touched = jnp.where(live, touched | (1 << target), touched)
                count = jnp.where(live, count + 1, count)
        tasks[line, 0] = count
        return touched

    for j in range(1 + 2 * rows):
        tasks[0, j] = 0
        tasks[steps + 1, j] = 0
    touched = lax.fori_loop(0, steps + 1, one_compute, jnp.int32(0))
    for k in range(supers):
        info[rows + k] = (touched >> (row * supers + k)) & 1
        other = jnp.int32(0)
        partner = lax.rem(row + 1, rows)
        for c in range(cols):
            other = other | (
                keep[k, partner * cols + c] & pattern[row * cols + col, partner * cols + c]
            )
        info[rows + supers + k] = other & keep[k, row * cols + col]
    for store in stores:
        store.wait()


def make_plan(place, pattern, keep, factor, rows, cols, steps):
    supers = keep.shape[0]
    poles, _, block_rows, width = factor.shape
    piece = (poles, 2, block_rows, width // supers)
    return pl.pallas_call(
        functools.partial(plan_kernel, rows, cols, supers, steps),
        out_shape=(
            jax.ShapeDtypeStruct((rows + 2 * supers + 1,), jnp.int32),
            jax.ShapeDtypeStruct((4, steps + 1), jnp.int32),
            jax.ShapeDtypeStruct((steps + 2, 1 + 2 * rows), jnp.int32),
            jax.ShapeDtypeStruct((supers * cols,) + piece, jnp.float32),
            jax.ShapeDtypeStruct(piece, jnp.float32),
            jax.ShapeDtypeStruct(piece, jnp.float32),
            jax.ShapeDtypeStruct((rows, poles, 2, block_rows, width), jnp.float32),
        ),
        in_specs=[smem(), smem(), smem(), anywhere()],
        out_specs=(smem(), smem(), smem(), anywhere(), anywhere(), anywhere(), anywhere()),
        scratch_shapes=[
            pltpu.VMEM((supers,) + piece, jnp.float32),
            pltpu.SemaphoreType.DMA((supers,)),
            pltpu.SemaphoreType.DMA((supers,)),
        ],
        compiler_params=pltpu.CompilerParams(vmem_limit_bytes=VMEM_BYTES),
        name="plan",
    )(place, pattern, keep, factor)


def route_kernel(
    step, moves, pool_in, arrive_up, arrive_down, pool, send_up, send_down,
    stage, load_sems, store_sems, send_sems,
):
    t = step[0]
    before = jnp.maximum(t - 1, 0)
    work = []
    for j, (arrived, leaving) in enumerate(((arrive_up, send_up), (arrive_down, send_down))):
        got = jnp.where(t > 0, moves[2 + j, before], -1)
        out = moves[j, t]
        fresh = (out >= 0) & (out == got)
        held = (out >= 0) & (out != got)
        load_held = pltpu.make_async_copy(
            pool.at[jnp.maximum(out, 0)], stage.at[2 + j], load_sems.at[2 + j]
        )
        load_got = pltpu.make_async_copy(arrived, stage.at[j], load_sems.at[j])
        send_held = pltpu.make_async_copy(stage.at[2 + j], leaving, send_sems.at[j])
        send_got = pltpu.make_async_copy(stage.at[j], leaving, send_sems.at[j])
        store = pltpu.make_async_copy(
            stage.at[j], pool.at[jnp.maximum(got, 0)], store_sems.at[j]
        )
        work.append((got >= 0, fresh, held, load_held, load_got, send_held, send_got, store))

    for _, _, held, load_held, _, _, _, _ in work:
        pl.when(held)(load_held.start)
    for come, _, _, _, load_got, _, _, _ in work:
        pl.when(come)(load_got.start)
    for _, _, held, load_held, _, send_held, _, _ in work:

        @pl.when(held)
        def _():
            load_held.wait()
            send_held.start()

    for come, fresh, _, _, load_got, _, send_got, store in work:

        @pl.when(come)
        def _():
            load_got.wait()
            pl.when(fresh)(send_got.start)
            store.start()

    for come, fresh, held, _, _, send_held, send_got, store in work:
        pl.when(held)(send_held.wait)
        pl.when(fresh)(send_got.wait)
        pl.when(come)(store.wait)


def route(step, moves, pool, arrive_up, arrive_down):
    piece = jax.ShapeDtypeStruct(arrive_up.shape, jnp.float32)
    return pl.pallas_call(
        route_kernel,
        out_shape=(jax.ShapeDtypeStruct(pool.shape, jnp.float32), piece, piece),
        in_specs=[smem(), smem(), anywhere(), anywhere(), anywhere()],
        out_specs=(anywhere(), anywhere(), anywhere()),
        input_output_aliases={2: 0},
        scratch_shapes=[
            pltpu.VMEM((4,) + arrive_up.shape, jnp.float32),
            pltpu.SemaphoreType.DMA((4,)),
            pltpu.SemaphoreType.DMA((2,)),
            pltpu.SemaphoreType.DMA((2,)),
        ],
        compiler_params=pltpu.CompilerParams(vmem_limit_bytes=VMEM_BYTES),
        name="route",
    )(step, moves, pool, arrive_up, arrive_down)


def tile_kernel(poles, step, tasks, tile, piece, total_in, total, left_hi, left_lo, right_hi, right_lo):
    position = pl.program_id(0)
    each = tasks[step[0], 0]
    count = each * poles
    last = jnp.maximum(each - 1, 0)
    code = tasks[step[0], 1 + jnp.minimum(lax.rem(position, jnp.maximum(each, 1)), last)]
    first = (code // 65536) % 2
    joined = code // 131072
    rows, depth = tile.shape[3], tile.shape[4]
    width = piece.shape[4]

    @pl.when((position == 0) & (count == 0))
    def _():
        total[...] = total_in[...]

    @pl.when(position < count)
    def _():
        @pl.when((joined == 0) & (first == 1))
        def _():
            total[...] = jnp.zeros_like(total)

        @pl.when((joined == 0) & (first == 0))
        def _():
            total[...] = total_in[...]

        for part in range(2):
            high, low = halves(tile[0, part, 0])
            left_hi[:, part * depth : (part + 1) * depth] = high
            left_lo[:, part * depth : (part + 1) * depth] = low
            high, low = halves(piece[0, 0, part])
            here = slice(part * depth, (part + 1) * depth)
            there = slice((1 - part) * depth, (2 - part) * depth)
            right_hi[here, :width] = high if part == 0 else -high
            right_lo[here, :width] = low if part == 0 else -low
            right_hi[there, width:] = high
            right_lo[there, width:] = low
        chunk = min(256, rows)
        for start in range(0, rows, chunk):
            span = slice(start, start + chunk)
            value = jnp.dot(
                left_hi[span, :], right_hi[...], preferred_element_type=jnp.float32
            )
            value += jnp.dot(
                left_hi[span, :], right_lo[...], preferred_element_type=jnp.float32
            )
            value += jnp.dot(
                left_lo[span, :], right_hi[...], preferred_element_type=jnp.float32
            )
            total[0, 0, 0, span, :] += value[:, :width]
            total[0, 0, 1, span, :] += value[:, width:]


def add_tiles(step, tasks, tiles, pool, total, cols):
    poles, _, rows, block_rows, _ = tiles.shape
    piece_cols = pool.shape[4]

    def task_of(i, step, tasks):
        each = tasks[step[0], 0]
        spot = jnp.minimum(i, jnp.maximum(each * poles - 1, 0))
        q = lax.div(spot, jnp.maximum(each, 1))
        return q, tasks[step[0], 1 + spot - q * each]

    def tile_at(i, step, tasks):
        q, code = task_of(i, step, tasks)
        return q, 0, (code // 256) % 16, 0, (code % 256) % cols

    def piece_at(i, step, tasks):
        q, code = task_of(i, step, tasks)
        return code % 256, q, 0, 0, 0

    def total_at(i, step, tasks):
        q, code = task_of(i, step, tasks)
        return (code // 4096) % 16, q, 0, 0, (code % 256) // cols

    total_spec = pl.BlockSpec((1, 1, 2, block_rows, piece_cols), total_at)
    return pl.pallas_call(
        functools.partial(tile_kernel, poles),
        out_shape=jax.ShapeDtypeStruct(total.shape, jnp.float32),
        grid_spec=pltpu.PrefetchScalarGridSpec(
            num_scalar_prefetch=2,
            grid=(poles * 2 * rows,),
            in_specs=[
                pl.BlockSpec((1, 2, 1, block_rows, block_rows), tile_at),
                pl.BlockSpec((1, 1, 2, block_rows, piece_cols), piece_at),
                total_spec,
            ],
            out_specs=total_spec,
            scratch_shapes=[
                pltpu.VMEM((block_rows, 2 * block_rows), BF16),
                pltpu.VMEM((block_rows, 2 * block_rows), BF16),
                pltpu.VMEM((2 * block_rows, 2 * piece_cols), BF16),
                pltpu.VMEM((2 * block_rows, 2 * piece_cols), BF16),
            ],
        ),
        input_output_aliases={4: 0},
        compiler_params=pltpu.CompilerParams(
            dimension_semantics=("arbitrary",), vmem_limit_bytes=VMEM_BYTES
        ),
        cost_estimate=pl.CostEstimate(
            flops=poles * 6 * 8 * block_rows * block_rows * piece_cols,
            bytes_accessed=poles * 3 * 16 * block_rows * block_rows,
            transcendentals=0,
        ),
        name="tiles",
    )(step, tasks, tiles, pool, total)


def finish_kernel(
    owners, place, info, order, table, owner_row, own, other, factor, diag,
    result, *rest,
):
    packed, parts = rest[:owners], rest[owners : 2 * owners]
    dens, slot, block = rest[2 * owners :]
    rows, cols, supers = place[3], place[4], place[5]
    k, q = pl.program_id(0), pl.program_id(1)
    poles = pl.num_programs(1)
    height = own.shape[3]
    own_live = info[rows + k] != 0
    other_live = info[rows + supers + k] != 0
    pole = order[place[2] * poles + q]
    real, imag = table[pole, 0], table[pole, 1]

    @pl.when((k == 0) & (q == 0))
    def _():
        owner = owner_row[...]
        hot = lax.broadcasted_iota(jnp.int32, (8 * ((owners + 7) // 8), height), 0) == owner
        hot = hot.astype(jnp.float32)
        before = lax.broadcasted_iota(jnp.int32, (height, height), 0) < (
            lax.broadcasted_iota(jnp.int32, (height, height), 1)
        )
        ahead = jnp.dot(
            hot.astype(BF16), before.astype(jnp.float32).astype(BF16),
            preferred_element_type=jnp.float32,
        )
        slot[0:1, :] = jnp.sum(hot * ahead, axis=0, keepdims=True).astype(jnp.int32)
        slot[1:2, :] = owner ^ place[2]

    zero = jnp.zeros(own.shape[3:], jnp.float32)
    y_real = jnp.where(own_live, own[0, 0, 0], zero) + jnp.where(other_live, other[0, 0], zero)
    y_imag = jnp.where(own_live, own[0, 0, 1], zero) + jnp.where(other_live, other[0, 1], zero)
    result[0, 0] = y_real
    result[0, 1] = y_imag
    first = real * y_imag + imag * y_real
    second = real * y_real - imag * y_imag
    start = jnp.where(place[0] * cols + place[1] == 0, 1.0, 0.0)
    term = start * (real * diag[0, 1, 0] + imag * diag[0, 0, 0])

    @pl.when(q == 0)
    def _():
        dens[...] = first
        block[k] = term

    @pl.when(q > 0)
    def _():
        dens[...] += first
        block[k] += term

    @pl.when(own_live | other_live)
    def _():
        for left, right in ((factor[0, 0], first), (factor[0, 1], second)):
            left_hi, left_lo = halves(left)
            right_hi, right_lo = halves(right)
            for a, b in ((left_hi, right_hi), (left_hi, right_lo), (left_lo, right_hi)):
                block[k] -= lax.dot_general(
                    a, b, (((0,), (0,)), ((), ())), preferred_element_type=jnp.float32
                )

    @pl.when(q == poles - 1)
    def _():
        high, low = halves(dens[...])
        for d in range(owners):
            capacity = packed[d].shape[0]
            mine = lax.broadcasted_iota(jnp.int32, (capacity, height), 0) == slot[0:1, :]
            mine = mine & (slot[1:2, :] == d)
            pick = mine.astype(jnp.float32).astype(BF16)
            packed[d][...] = jnp.dot(
                pick, high, preferred_element_type=jnp.float32
            ) + jnp.dot(pick, low, preferred_element_type=jnp.float32)

    @pl.when((q == poles - 1) & (k == pl.num_programs(0) - 1))
    def _():
        height = parts[0].shape[0]
        share = block.shape[1] // height
        for d in range(owners):
            part = place[2] ^ d
            start = pl.multiple_of((part % share) * height, height)
            parts[d][...] = block[part // share, pl.ds(start, height), :]


def finish(place, info, order, table, owner_row, total, other, factor, diag, owners, supers):
    poles, _, block_rows, width = factor.shape
    columns = width // supers
    capacity = block_rows // 2
    part = supers * columns // owners
    flat = pl.BlockSpec((1, 2, block_rows, columns), lambda k, q: (q, 0, 0, k))
    return pl.pallas_call(
        functools.partial(finish_kernel, owners),
        out_shape=(
            jax.ShapeDtypeStruct(factor.shape, jnp.float32),
        )
        + (jax.ShapeDtypeStruct((capacity, width), jnp.float32),) * owners
        + (jax.ShapeDtypeStruct((part, columns), jnp.float32),) * owners,
        grid=(supers, poles),
        in_specs=[smem(), smem(), smem(), smem()]
        + [
            pl.BlockSpec((1, block_rows), lambda k, q: (0, 0)),
            pl.BlockSpec((1, 1, 2, block_rows, columns), lambda k, q: (0, q, 0, 0, k)),
            flat,
            flat,
            pl.BlockSpec((1, 2, 1, columns, columns), lambda k, q: (q, 0, k, 0, 0)),
        ],
        out_specs=(flat,)
        + (pl.BlockSpec((capacity, columns), lambda k, q: (0, k)),) * owners
        + (pl.BlockSpec((part, columns), lambda k, q: (0, 0)),) * owners,
        scratch_shapes=[
            pltpu.VMEM((block_rows, columns), jnp.float32),
            pltpu.VMEM((8, block_rows), jnp.int32),
            pltpu.VMEM((supers, columns, columns), jnp.float32),
        ],
        compiler_params=pltpu.CompilerParams(
            dimension_semantics=("arbitrary", "arbitrary"), vmem_limit_bytes=VMEM_BYTES
        ),
        name="finish",
    )(place, info, order, table, owner_row, total, other, factor, diag)


def swap(value, axis, size, distance):
    return lax.ppermute(value, axis, [(i, i ^ distance) for i in range(size)])


def sum_xor(values, axis, size):
    terms = [values[0]] + [swap(values[d], axis, size, d) for d in range(1, size)]
    while len(terms) > 1:
        terms = [a + b for a, b in zip(terms[::2], terms[1::2])]
    return terms[0]


def arrange_kernel(place, *refs):
    parts, out = refs[:-1], refs[-1]
    height = parts[0].shape[0]
    for d, part in enumerate(parts):
        start = pl.multiple_of((place[2] ^ d) * height, height)
        out[pl.ds(start, height), :] = part[...]


def arrange(place, parts):
    height, width = parts[0].shape
    return pl.pallas_call(
        arrange_kernel,
        out_shape=jax.ShapeDtypeStruct((height * len(parts), width), jnp.float32),
        in_specs=[smem()] + [pl.BlockSpec(memory_space=pltpu.VMEM)] * len(parts),
        out_specs=pl.BlockSpec(memory_space=pltpu.VMEM),
        name="arrange",
    )(place, *parts)


def sparse_shards(
    inverse_tiles, factor_block, diag_inverse, tile_pattern, ancestor_blocks, row_owner,
    pole_weights, pole_order,
):
    rows = lax.axis_size("row")
    cols = lax.axis_size("col")
    owners = lax.axis_size("pole")
    supers = ancestor_blocks.shape[0]
    block_rows, width = factor_block.shape[2:]
    steps = supers * cols * (cols - 1) // 2
    place = jnp.stack(
        [
            lax.axis_index("row"), lax.axis_index("col"), lax.axis_index("pole"),
            jnp.int32(rows), jnp.int32(cols), jnp.int32(supers),
        ]
    ).astype(jnp.int32)
    info, moves, tasks, pool, arrive_up, arrive_down, total = make_plan(
        place, tile_pattern, ancestor_blocks, factor_block, rows, cols, steps
    )
    ends = [info[r] for r in range(rows)]

    def advance(members):
        up = [(r * cols + c, r * cols + c + 1) for r in members for c in range(cols - 1)]
        down = [(b, a) for a, b in up]

        def body(state):
            t, pool, total, arrive_up, arrive_down = state
            step = t[None]
            pool, send_up, send_down = route(step, moves, pool, arrive_up, arrive_down)
            arrive_up = lax.ppermute(send_up, ("row", "col"), up)
            arrive_down = lax.ppermute(send_down, ("row", "col"), down)
            total = add_tiles(step, tasks, inverse_tiles, pool, total, cols)
            return t + 1, pool, total, arrive_up, arrive_down

        return body

    total = lax.cond(
        info[rows + 2 * supers] != 0,
        lambda held: add_tiles(
            jnp.full((1,), steps + 1, jnp.int32), tasks, inverse_tiles, pool, held, cols
        ),
        lambda held: held,
        total,
    )
    state = (jnp.int32(0), pool, total, arrive_up, arrive_down)
    shortest = functools.reduce(jnp.minimum, ends)
    state = lax.while_loop(lambda s: s[0] < shortest, advance(range(rows)), state)
    for r in range(rows):
        state = lax.while_loop(lambda s, r=r: s[0] < ends[r], advance([r]), state)
    t, pool, total, arrive_up, arrive_down = state
    step = t[None]
    pool, _, _ = route(step, moves, pool, arrive_up, arrive_down)
    total = add_tiles(step, tasks, inverse_tiles, pool, total, cols)
    other = lax.ppermute(total[1], "row", [(0, 1), (1, 0)])
    inverse_rows, *sums = finish(
        place, info, pole_order, pole_weights, row_owner.reshape(1, block_rows), total, other,
        factor_block, diag_inverse, owners, supers,
    )
    packed, parts = sums[:owners], sums[owners:]
    part = sum_xor(parts, "pole", owners)
    part = sum_xor([part] * rows, "row", rows)
    part = sum_xor([part] * cols, "col", cols)
    whole = [part] + [swap(part, "pole", owners, d) for d in range(1, owners)]
    block_density = arrange(place, whole).reshape(supers, width // supers, width // supers)
    owned = sum_xor(packed, "pole", owners)
    return inverse_rows, owned[None], block_density


def product_high(left, right):
    return jnp.einsum("pts,psw->ptw", left, right, precision=lax.Precision.HIGHEST)


def contract(first, second):
    return jnp.einsum("pbks,pbkt->pkst", first, second, precision=lax.Precision.HIGHEST)


def shards(
    inverse_tiles,
    factor_block,
    diag_inverse,
    tile_pattern,
    ancestor_blocks,
    row_owner,
    pole_weights,
    pole_order,
):
    row_count = lax.axis_size("row")
    col_count = lax.axis_size("col")
    pole_total = lax.axis_size("pole")
    row_index = lax.axis_index("row")
    col_index = lax.axis_index("col")
    pole_index = lax.axis_index("pole")
    pole_count = inverse_tiles.shape[0]
    block_rows = inverse_tiles.shape[3]
    seg_cols = inverse_tiles.shape[4]
    width = factor_block.shape[3]
    supers = ancestor_blocks.shape[0]
    super_cols = width // supers
    own_block = row_index * col_count + col_index
    pattern_grid = tile_pattern.reshape(row_count, col_count, row_count, col_count).astype(
        jnp.float32
    )
    rows_pick = lax.dynamic_index_in_dim(pattern_grid, col_index, 1, keepdims=False)
    tiles_here = lax.dynamic_index_in_dim(rows_pick, row_index, 1, keepdims=False)
    col_keep = jnp.repeat(tiles_here, block_rows, axis=1)
    masked = inverse_tiles * col_keep[None, None, :, None, :]
    flattened = masked.reshape(pole_count, 2, row_count * block_rows, seg_cols)
    anc_keep = lax.dynamic_index_in_dim(ancestor_blocks, own_block, 1, keepdims=False).astype(
        jnp.float32
    )
    width_keep = jnp.repeat(anc_keep, super_cols)
    factor = factor_block * width_keep
    fac_piece = lax.all_gather(factor, "col", axis=2, tiled=True)
    real_part = product_high(flattened[:, 0], fac_piece[:, 0]) - product_high(
        flattened[:, 1], fac_piece[:, 1]
    )
    imag_part = product_high(flattened[:, 0], fac_piece[:, 1]) + product_high(
        flattened[:, 1], fac_piece[:, 0]
    )
    partial_value = jnp.stack([real_part, imag_part], axis=1)
    inverse_rows = (
        lax.psum_scatter(partial_value, "row", scatter_dimension=2, tiled=True) * width_keep
    )
    fac_split = factor.reshape(pole_count, 2, block_rows, supers, super_cols)
    rows_split = inverse_rows.reshape(pole_count, 2, block_rows, supers, super_cols)
    prod_real = contract(fac_split[:, 0], rows_split[:, 0]) - contract(
        fac_split[:, 1], rows_split[:, 1]
    )
    prod_imag = contract(fac_split[:, 0], rows_split[:, 1]) + contract(
        fac_split[:, 1], rows_split[:, 0]
    )
    order_here = lax.dynamic_slice_in_dim(pole_order, pole_index * pole_count, pole_count)
    table_hot = (
        order_here[:, None] == jnp.arange(pole_order.shape[0], dtype=jnp.int32)[None, :]
    ).astype(jnp.float32)
    weights = jnp.dot(
        table_hot, pole_weights, precision=lax.Precision.HIGHEST, preferred_element_type=jnp.float32
    )
    weight_real = weights[:, 0]
    weight_imag = weights[:, 1]
    summed_real, summed_imag = lax.psum((prod_real, prod_imag), ("row", "col"))
    green_real = diag_inverse[:, 0] - summed_real
    green_imag = diag_inverse[:, 1] - summed_imag
    local_kk = jnp.sum(
        weight_real[:, None, None, None] * green_imag
        + weight_imag[:, None, None, None] * green_real,
        axis=0,
    )
    block_density = lax.psum(local_kk, "pole")
    dens_local = jnp.sum(
        weight_real[:, None, None] * inverse_rows[:, 1]
        + weight_imag[:, None, None] * inverse_rows[:, 0],
        axis=0,
    )
    owner_ids = row_owner[:, 0]
    owner_hot = (owner_ids[:, None] == jnp.arange(pole_total, dtype=jnp.int32)[None, :]).astype(
        jnp.int32
    )
    owner_rank = jnp.cumsum(owner_hot, axis=0) - owner_hot
    rank_own = jnp.sum(owner_hot * owner_rank, axis=1)
    capacity = block_rows // 2
    slot_hit = (rank_own[:, None] == jnp.arange(capacity, dtype=jnp.int32)[None, :]).astype(
        jnp.float32
    )
    selector = jnp.transpose(
        owner_hot.astype(jnp.float32)[:, :, None] * slot_hit[:, None, :], (1, 2, 0)
    )
    summed_rows = lax.psum(dens_local, "pole")
    my_select = lax.dynamic_index_in_dim(selector, pole_index, 0, keepdims=True)
    owned_density = jnp.einsum(
        "pst,tw->psw", my_select, summed_rows, precision=lax.Precision.HIGHEST
    )
    return (inverse_rows, owned_density, block_density)


def solution(mesh):
    placed = (
        P("pole", None, None, "col", "row"),
        P("pole", None, ("row", "col"), None),
        P("pole", None, None, None, None),
        P(),
        P(),
        P(("row", "col"), None),
        P(),
        P(),
    )
    sizes = dict(mesh.shape)
    line_ok = sizes["row"] == 2 and sizes["col"] in (2, 4, 8) and sizes["pole"] in (1, 2, 4, 8)

    def chosen(inverse_tiles, factor_block, *rest):
        tiled = factor_block.shape[2] % 256 == 0 and rest[2].shape[0] == 2
        run = sparse_shards if line_ok and tiled else shards
        return run(inverse_tiles, factor_block, *rest)

    return jax.shard_map(
        chosen,
        mesh=mesh,
        in_specs=placed,
        out_specs=(P("pole", None, ("row", "col"), None), P("pole", ("row", "col"), None), P()),
        check_vma=False,
    )
```

```python
import functools

import jax
import jax.numpy as jnp
from jax import lax
from jax.experimental import pallas as pl
from jax.experimental.pallas import tpu as pltpu
from jax.sharding import PartitionSpec as P

BF16 = jnp.bfloat16
VMEM_BYTES = 60 * 1024 * 1024


def smem():
    return pl.BlockSpec(memory_space=pltpu.SMEM)


def anywhere():
    return pl.BlockSpec(memory_space=pl.ANY)


def halves(value):
    high = value.astype(BF16)
    return high, (value - high.astype(jnp.float32)).astype(BF16)


def lowest_of(mask):
    return mask & -mask


def piece_index(bit, pieces):
    index = jnp.int32(-1)
    for i in range(pieces):
        index = jnp.where(bit == (1 << i), i, index)
    return index


def plan_kernel(
    rows, cols, supers, steps, place, pattern, keep, factor,
    info, moves, tasks, pool, arrive_up, arrive_down, total, stage, load_sems, store_sems,
):
    row, col = place[0], place[1]
    width = factor.shape[3] // supers
    pieces = supers * cols
    loads = [
        pltpu.make_async_copy(
            factor.at[:, :, :, pl.ds(k * width, width)], stage.at[k], load_sems.at[k]
        )
        for k in range(supers)
    ]
    stores = [
        pltpu.make_async_copy(stage.at[k], pool.at[k * cols + col], store_sems.at[k])
        for k in range(supers)
    ]
    for load in loads:
        load.start()
    for load, store in zip(loads, stores):
        load.wait()
        store.start()
    source = [sum(1 << i for i in range(c, pieces, cols)) for c in range(cols)]
    links = cols - 1

    def one_row(i, carry):
        r = lax.rem(row + 1 + i, rows)
        kept = jnp.int32(0)
        for k in range(supers):
            for c in range(cols):
                kept = kept | (keep[k, r * cols + c] << (k * cols + c))
        need = []
        for c2 in range(cols):
            mask = jnp.int32(0)
            for g in range(rows):
                bits = jnp.int32(0)
                for c in range(cols):
                    bits = bits | (pattern[g * cols + c2, r * cols + c] << c)
                for k in range(supers):
                    mask = mask | ((keep[k, g * cols + c2] * bits) << (k * cols))
            need.append(mask & kept & ~source[c2])
        up_need, down_need = [], []
        for l in range(links):
            above = functools.reduce(lambda a, b: a | b, need[l + 1 :])
            below = functools.reduce(lambda a, b: a | b, need[: l + 1])
            up_need.append(above & sum(source[: l + 1]))
            down_need.append(below & sum(source[l + 1 :]))

        def one_step(state):
            t, up_left, up_have, down_left, down_have = state
            up_bit, down_bit = [], []
            for l in range(links):
                ready = up_left[l] & up_have[l]
                pick = jnp.int32(0)
                for m in range(l, links):
                    part = ready & up_need[m]
                    pick = jnp.where(part != 0, part, pick)
                up_bit.append(lowest_of(pick))
                ready = down_left[l] & down_have[l + 1]
                pick = jnp.int32(0)
                for m in range(l, -1, -1):
                    part = ready & down_need[m]
                    pick = jnp.where(part != 0, part, pick)
                down_bit.append(lowest_of(pick))
            up_left = [left ^ bit for left, bit in zip(up_left, up_bit)]
            down_left = [left ^ bit for left, bit in zip(down_left, down_bit)]
            up_have = up_have[:1] + [have | bit for have, bit in zip(up_have[1:], up_bit)]
            down_have = [have | bit for have, bit in zip(down_have, down_bit)] + down_have[-1:]
            none = jnp.int32(0)
            send_up = sum([jnp.where(col == l, up_bit[l], none) for l in range(links)])
            send_down = sum([jnp.where(col == l + 1, down_bit[l], none) for l in range(links)])
            get_up = sum([jnp.where(col == l + 1, up_bit[l], none) for l in range(links)])
            get_down = sum([jnp.where(col == l, down_bit[l], none) for l in range(links)])
            for j, bit in enumerate((send_up, send_down, get_up, get_down)):
                moves[j, t] = piece_index(bit, pieces)
            return t + 1, up_left, up_have, down_left, down_have

        own = [jnp.int32(s) for s in source]

        def clear(t, done):
            for j in range(4):
                moves[j, t] = -1
            return done

        def unfinished(state):
            return functools.reduce(lambda a, b: a | b, state[1] + state[3]) != 0

        lax.fori_loop(0, steps + 1, clear, jnp.int32(0))
        state = (jnp.int32(0), up_need, own, down_need, own)
        info[r] = lax.while_loop(unfinished, one_step, state)[0]
        return carry

    lax.fori_loop(0, rows, one_row, jnp.int32(0))
    shortest, longest = info[row], info[row]
    for r in range(rows):
        shortest = jnp.minimum(shortest, info[r])
        longest = jnp.maximum(longest, info[r])
    ahead = jnp.int32(0)
    for r in range(rows):
        ahead = ahead | jnp.where(info[r] > info[row], 1, 0)
    early = jnp.where(shortest > 0, ahead, 0)
    info[rows + 2 * supers] = early

    def one_compute(s, touched):
        line = jnp.where((s == 0) & (early != 0), steps + 1, s)
        before = jnp.maximum(s - 1, 0)
        items = []
        for j in range(2):
            item = jnp.where(keep[j, row * cols + col] != 0, j * cols + col, -1)
            items.append(jnp.where(s == 0, item, moves[2 + j, before]))
        count = jnp.int32(0)
        previous = jnp.int32(-1)
        for j in range(1 + 2 * rows):
            tasks[line, j] = 0
        for g in range(rows):
            relative = lax.rem(g - row + rows, rows)
            for item in items:
                safe = jnp.maximum(item, 0)
                k = safe // cols
                c = safe - k * cols
                live = (
                    (item >= 0)
                    & (keep[k, g * cols + col] != 0)
                    & (pattern[g * cols + col, row * cols + c] != 0)
                )
                target = g * supers + k
                seen = (touched >> target) & 1
                joined = jnp.where(previous == target, 1, 0)
                code = (
                    safe + g * 256 + relative * 4096 + (1 - seen) * 65536 + joined * 131072
                )

                @pl.when(live)
                def _():
                    tasks[line, 1 + count] = code

                previous = jnp.where(live, target, previous)
                touched = jnp.where(live, touched | (1 << target), touched)
                count = jnp.where(live, count + 1, count)
        tasks[line, 0] = count
        return touched

    for j in range(1 + 2 * rows):
        tasks[0, j] = 0
        tasks[steps + 1, j] = 0
    touched = lax.fori_loop(0, longest + 1, one_compute, jnp.int32(0))
    for k in range(supers):
        info[rows + k] = (touched >> (row * supers + k)) & 1
        other = jnp.int32(0)
        partner = lax.rem(row + 1, rows)
        for c in range(cols):
            other = other | (
                keep[k, partner * cols + c] & pattern[row * cols + col, partner * cols + c]
            )
        info[rows + supers + k] = other & keep[k, row * cols + col]
    for store in stores:
        store.wait()


def make_plan(place, pattern, keep, factor, rows, cols, steps):
    supers = keep.shape[0]
    poles, _, block_rows, width = factor.shape
    piece = (poles, 2, block_rows, width // supers)
    return pl.pallas_call(
        functools.partial(plan_kernel, rows, cols, supers, steps),
        out_shape=(
            jax.ShapeDtypeStruct((rows + 2 * supers + 1,), jnp.int32),
            jax.ShapeDtypeStruct((4, steps + 1), jnp.int32),
            jax.ShapeDtypeStruct((steps + 2, 1 + 2 * rows), jnp.int32),
            jax.ShapeDtypeStruct((supers * cols,) + piece, jnp.float32),
            jax.ShapeDtypeStruct(piece, jnp.float32),
            jax.ShapeDtypeStruct(piece, jnp.float32),
            jax.ShapeDtypeStruct((rows, supers) + piece, jnp.float32),
        ),
        in_specs=[smem(), smem(), smem(), anywhere()],
        out_specs=(smem(), smem(), smem(), anywhere(), anywhere(), anywhere(), anywhere()),
        scratch_shapes=[
            pltpu.VMEM((supers,) + piece, jnp.float32),
            pltpu.SemaphoreType.DMA((supers,)),
            pltpu.SemaphoreType.DMA((supers,)),
        ],
        compiler_params=pltpu.CompilerParams(vmem_limit_bytes=VMEM_BYTES),
        name="plan",
    )(place, pattern, keep, factor)


def route_kernel(
    step, moves, pool_in, arrive_up, arrive_down, pool, send_up, send_down,
    stage, load_sems, store_sems, send_sems,
):
    t = step[0]
    before = jnp.maximum(t - 1, 0)
    work = []
    for j, (arrived, leaving) in enumerate(((arrive_up, send_up), (arrive_down, send_down))):
        got = jnp.where(t > 0, moves[2 + j, before], -1)
        out = moves[j, t]
        fresh = (out >= 0) & (out == got)
        held = (out >= 0) & (out != got)
        load_held = pltpu.make_async_copy(
            pool.at[jnp.maximum(out, 0)], stage.at[2 + j], load_sems.at[2 + j]
        )
        load_got = pltpu.make_async_copy(arrived, stage.at[j], load_sems.at[j])
        send_held = pltpu.make_async_copy(stage.at[2 + j], leaving, send_sems.at[j])
        send_got = pltpu.make_async_copy(stage.at[j], leaving, send_sems.at[j])
        store = pltpu.make_async_copy(
            stage.at[j], pool.at[jnp.maximum(got, 0)], store_sems.at[j]
        )
        work.append((got >= 0, fresh, held, load_held, load_got, send_held, send_got, store))

    for _, _, held, load_held, _, _, _, _ in work:
        pl.when(held)(load_held.start)
    for come, _, _, _, load_got, _, _, _ in work:
        pl.when(come)(load_got.start)
    for _, _, held, load_held, _, send_held, _, _ in work:

        @pl.when(held)
        def _():
            load_held.wait()
            send_held.start()

    for come, fresh, _, _, load_got, _, send_got, store in work:

        @pl.when(come)
        def _():
            load_got.wait()
            pl.when(fresh)(send_got.start)
            store.start()

    for come, fresh, held, _, _, send_held, send_got, store in work:
        pl.when(held)(send_held.wait)
        pl.when(fresh)(send_got.wait)
        pl.when(come)(store.wait)


def route(step, moves, pool, arrive_up, arrive_down):
    piece = jax.ShapeDtypeStruct(arrive_up.shape, jnp.float32)
    return pl.pallas_call(
        route_kernel,
        out_shape=(jax.ShapeDtypeStruct(pool.shape, jnp.float32), piece, piece),
        in_specs=[smem(), smem(), anywhere(), anywhere(), anywhere()],
        out_specs=(anywhere(), anywhere(), anywhere()),
        input_output_aliases={2: 0},
        scratch_shapes=[
            pltpu.VMEM((4,) + arrive_up.shape, jnp.float32),
            pltpu.SemaphoreType.DMA((4,)),
            pltpu.SemaphoreType.DMA((2,)),
            pltpu.SemaphoreType.DMA((2,)),
        ],
        compiler_params=pltpu.CompilerParams(vmem_limit_bytes=VMEM_BYTES),
        name="route",
    )(step, moves, pool, arrive_up, arrive_down)


def tile_kernel(
    poles, step, tasks, tile, piece, total_in, total, left_hi, left_lo, right_hi, right_lo,
):
    position = pl.program_id(0)
    each = tasks[step[0], 0]
    count = each * poles
    spot = jnp.minimum(position, jnp.maximum(count - 1, 0))
    code = tasks[step[0], 1 + spot - lax.div(spot, jnp.maximum(each, 1)) * each]
    first = (code // 65536) % 2
    joined = code // 131072
    rows, depth = tile.shape[3], tile.shape[4]
    width = piece.shape[4]

    @pl.when((position == 0) & (count == 0))
    def _():
        total[...] = total_in[...]

    @pl.when(position < count)
    def _():
        @pl.when((joined == 0) & (first == 1))
        def _():
            total[...] = jnp.zeros_like(total)

        @pl.when((joined == 0) & (first == 0))
        def _():
            total[...] = total_in[...]

        for part in range(2):
            high, low = halves(tile[0, part, 0])
            left_hi[:, part * depth : (part + 1) * depth] = high
            left_lo[:, part * depth : (part + 1) * depth] = low
            high, low = halves(piece[0, 0, part])
            here = slice(part * depth, (part + 1) * depth)
            there = slice((1 - part) * depth, (2 - part) * depth)
            right_hi[here, :width] = high if part == 0 else -high
            right_lo[here, :width] = low if part == 0 else -low
            right_hi[there, width:] = high
            right_lo[there, width:] = low
        chunk = min(256, rows)
        for start in range(0, rows, chunk):
            span = slice(start, start + chunk)
            value = jnp.dot(
                left_hi[span, :], right_hi[...], preferred_element_type=jnp.float32
            )
            value += jnp.dot(
                left_hi[span, :], right_lo[...], preferred_element_type=jnp.float32
            )
            value += jnp.dot(
                left_lo[span, :], right_hi[...], preferred_element_type=jnp.float32
            )
            total[0, 0, 0, 0, span, :] += value[:, :width]
            total[0, 0, 0, 1, span, :] += value[:, width:]


def add_tiles(step, tasks, tiles, pool, total, cols):
    poles, block_rows, piece_cols = total.shape[2], *total.shape[4:]
    slots = tasks.shape[1] - 1

    def task_of(i, step, tasks):
        each = tasks[step[0], 0]
        spot = jnp.minimum(i, jnp.maximum(each * poles - 1, 0))
        q = lax.div(spot, jnp.maximum(each, 1))
        return q, tasks[step[0], 1 + spot - q * each]

    def tile_at(i, step, tasks):
        q, code = task_of(i, step, tasks)
        return q, 0, (code // 256) % 16, 0, (code % 256) % cols

    def piece_at(i, step, tasks):
        q, code = task_of(i, step, tasks)
        return code % 256, q, 0, 0, 0

    def total_at(i, step, tasks):
        q, code = task_of(i, step, tasks)
        return (code // 4096) % 16, (code % 256) // cols, q, 0, 0, 0

    total_spec = pl.BlockSpec((1, 1, 1, 2, block_rows, piece_cols), total_at)
    return pl.pallas_call(
        functools.partial(tile_kernel, poles),
        out_shape=jax.ShapeDtypeStruct(total.shape, jnp.float32),
        grid_spec=pltpu.PrefetchScalarGridSpec(
            num_scalar_prefetch=2,
            grid=(poles * slots,),
            in_specs=[
                pl.BlockSpec((1, 2, 1, block_rows, block_rows), tile_at),
                pl.BlockSpec((1, 1, 2, block_rows, piece_cols), piece_at),
                total_spec,
            ],
            out_specs=total_spec,
            scratch_shapes=[
                pltpu.VMEM((block_rows, 2 * block_rows), BF16),
                pltpu.VMEM((block_rows, 2 * block_rows), BF16),
                pltpu.VMEM((2 * block_rows, 2 * piece_cols), BF16),
                pltpu.VMEM((2 * block_rows, 2 * piece_cols), BF16),
            ],
        ),
        input_output_aliases={4: 0},
        compiler_params=pltpu.CompilerParams(
            dimension_semantics=("arbitrary",), vmem_limit_bytes=VMEM_BYTES
        ),
        cost_estimate=pl.CostEstimate(
            flops=poles * 6 * 8 * block_rows * block_rows * piece_cols,
            bytes_accessed=poles * 3 * 16 * block_rows * block_rows,
            transcendentals=0,
        ),
        name="tiles",
    )(step, tasks, tiles, pool, total)


def finish_kernel(
    owners, k, supers, place, info, order, table, owner_row, own, other, factor, diag, *rest,
):
    last = k == supers - 1
    before, rest = (rest[1 : 1 + k], rest[1 + k :]) if k else ((), rest)
    result, packed, rest = rest[0], rest[1 : 1 + owners], rest[1 + owners :]
    sums, (dens, slot, block) = rest[:-3], rest[-3:]
    rows, cols = place[3], place[4]
    q = pl.program_id(0)
    poles = pl.num_programs(0)
    height = own.shape[4]
    own_live = info[rows + k] != 0
    other_live = info[rows + supers + k] != 0
    pole = order[place[2] * poles + q]
    real, imag = table[pole, 0], table[pole, 1]

    @pl.when(q == 0)
    def _():
        owner = owner_row[...]
        hot = lax.broadcasted_iota(jnp.int32, (8 * ((owners + 7) // 8), height), 0) == owner
        hot = hot.astype(jnp.float32)
        before_it = lax.broadcasted_iota(jnp.int32, (height, height), 0) < (
            lax.broadcasted_iota(jnp.int32, (height, height), 1)
        )
        ahead = jnp.dot(
            hot.astype(BF16), before_it.astype(jnp.float32).astype(BF16),
            preferred_element_type=jnp.float32,
        )
        slot[0:1, :] = jnp.sum(hot * ahead, axis=0, keepdims=True).astype(jnp.int32)
        slot[1:2, :] = owner ^ place[2]

    zero = jnp.zeros(own.shape[4:], jnp.float32)
    y_real = jnp.where(own_live, own[0, 0, 0, 0], zero) + jnp.where(other_live, other[0, 0], zero)
    y_imag = jnp.where(own_live, own[0, 0, 0, 1], zero) + jnp.where(other_live, other[0, 1], zero)
    result[0, 0] = y_real
    result[0, 1] = y_imag
    first = real * y_imag + imag * y_real
    second = real * y_real - imag * y_imag
    start = jnp.where(place[0] * cols + place[1] == 0, 1.0, 0.0)
    term = start * (real * diag[0, 1, 0] + imag * diag[0, 0, 0])

    @pl.when(q == 0)
    def _():
        dens[...] = first
        block[k] = term

    @pl.when(q > 0)
    def _():
        dens[...] += first
        block[k] += term

    @pl.when(own_live | other_live)
    def _():
        for left, right in ((factor[0, 0], first), (factor[0, 1], second)):
            left_hi, left_lo = halves(left)
            right_hi, right_lo = halves(right)
            for a, b in ((left_hi, right_hi), (left_hi, right_lo), (left_lo, right_hi)):
                block[k] -= lax.dot_general(
                    a, b, (((0,), (0,)), ((), ())), preferred_element_type=jnp.float32
                )

    @pl.when(q == poles - 1)
    def _():
        high, low = halves(dens[...])
        for d in range(owners):
            capacity = packed[d].shape[0]
            mine = lax.broadcasted_iota(jnp.int32, (capacity, height), 0) == slot[0:1, :]
            mine = mine & (slot[1:2, :] == d)
            pick = mine.astype(jnp.float32).astype(BF16)
            packed[d][...] = jnp.dot(
                pick, high, preferred_element_type=jnp.float32
            ) + jnp.dot(pick, low, preferred_element_type=jnp.float32)
        if last:
            for j, earlier in enumerate(before):
                block[j] = earlier[...]
            tall = sums[0].shape[0]
            share = block.shape[1] // tall
            for d in range(owners):
                part = place[2] ^ d
                at = pl.multiple_of((part % share) * tall, tall)
                sums[d][...] = block[part // share, pl.ds(at, tall), :]
        else:
            sums[0][...] = block[k]


def finish(k, place, info, order, table, owner_row, total, other, factor, diag, earlier, owners):
    poles, _, block_rows, width = factor.shape
    supers = diag.shape[2]
    columns = width // supers
    capacity = block_rows // 2
    last = k == supers - 1
    piece = pl.BlockSpec((1, 2, block_rows, columns), lambda q: (q, 0, 0, k))
    square = jax.ShapeDtypeStruct((columns, columns), jnp.float32)
    part = jax.ShapeDtypeStruct((supers * columns // owners, columns), jnp.float32)
    sums = (part,) * owners if last else (square,)
    fixed = lambda shape: pl.BlockSpec(shape.shape, lambda q: (0,) * len(shape.shape))
    packed = jax.ShapeDtypeStruct((capacity, columns), jnp.float32)
    return pl.pallas_call(
        functools.partial(finish_kernel, owners, k, supers),
        out_shape=(jax.ShapeDtypeStruct(factor.shape, jnp.float32),)
        + (packed,) * owners
        + sums,
        grid=(poles,),
        in_specs=[smem(), smem(), smem(), smem()]
        + [
            pl.BlockSpec((1, block_rows), lambda q: (0, 0)),
            pl.BlockSpec((1, 1, 1, 2, block_rows, columns), lambda q: (0, k, q, 0, 0, 0)),
            pl.BlockSpec((1, 2, block_rows, columns), lambda q: (q, 0, 0, 0)),
            piece,
            pl.BlockSpec((1, 2, 1, columns, columns), lambda q: (q, 0, k, 0, 0)),
        ]
        + ([anywhere()] + [fixed(square)] * k if k else []),
        out_specs=(piece,) + (fixed(packed),) * owners + tuple(fixed(shape) for shape in sums),
        scratch_shapes=[
            pltpu.VMEM((block_rows, columns), jnp.float32),
            pltpu.VMEM((8, block_rows), jnp.int32),
            pltpu.VMEM((supers, columns, columns), jnp.float32),
        ],
        input_output_aliases={9: 0} if k else {},
        compiler_params=pltpu.CompilerParams(
            dimension_semantics=("arbitrary",), vmem_limit_bytes=VMEM_BYTES
        ),
        name="finish",
    )(place, info, order, table, owner_row, total, other, factor, diag, *earlier)


def swap(value, axis, size, distance):
    return lax.ppermute(value, axis, [(i, i ^ distance) for i in range(size)])


def sum_xor(values, axis, size):
    terms = [values[0]] + [swap(values[d], axis, size, d) for d in range(1, size)]
    while len(terms) > 1:
        terms = [a + b for a, b in zip(terms[::2], terms[1::2])]
    return terms[0]


def arrange_kernel(place, *refs):
    parts, out = refs[:-1], refs[-1]
    height = parts[0].shape[0]
    for d, part in enumerate(parts):
        start = pl.multiple_of((place[2] ^ d) * height, height)
        out[pl.ds(start, height), :] = part[...]


def arrange(place, parts):
    height, width = parts[0].shape
    return pl.pallas_call(
        arrange_kernel,
        out_shape=jax.ShapeDtypeStruct((height * len(parts), width), jnp.float32),
        in_specs=[smem()] + [pl.BlockSpec(memory_space=pltpu.VMEM)] * len(parts),
        out_specs=pl.BlockSpec(memory_space=pltpu.VMEM),
        name="arrange",
    )(place, *parts)


def sparse_shards(
    inverse_tiles, factor_block, diag_inverse, tile_pattern, ancestor_blocks, row_owner,
    pole_weights, pole_order,
):
    rows = lax.axis_size("row")
    cols = lax.axis_size("col")
    owners = lax.axis_size("pole")
    supers = ancestor_blocks.shape[0]
    block_rows, width = factor_block.shape[2:]
    steps = supers * cols * (cols - 1) // 2
    place = jnp.stack(
        [
            lax.axis_index("row"), lax.axis_index("col"), lax.axis_index("pole"),
            jnp.int32(rows), jnp.int32(cols), jnp.int32(supers),
        ]
    ).astype(jnp.int32)
    info, moves, tasks, pool, arrive_up, arrive_down, total = make_plan(
        place, tile_pattern, ancestor_blocks, factor_block, rows, cols, steps
    )
    ends = [info[r] for r in range(rows)]

    def advance(members):
        up = [(r * cols + c, r * cols + c + 1) for r in members for c in range(cols - 1)]
        down = [(b, a) for a, b in up]

        def body(state):
            t, pool, total, arrive_up, arrive_down = state
            step = t[None]
            pool, send_up, send_down = route(step, moves, pool, arrive_up, arrive_down)
            arrive_up = lax.ppermute(send_up, ("row", "col"), up)
            arrive_down = lax.ppermute(send_down, ("row", "col"), down)
            total = add_tiles(step, tasks, inverse_tiles, pool, total, cols)
            return t + 1, pool, total, arrive_up, arrive_down

        return body

    total = lax.cond(
        info[rows + 2 * supers] != 0,
        lambda held: add_tiles(
            jnp.full((1,), steps + 1, jnp.int32), tasks, inverse_tiles, pool, held, cols
        ),
        lambda held: held,
        total,
    )
    state = (jnp.int32(0), pool, total, arrive_up, arrive_down)
    shortest = functools.reduce(jnp.minimum, ends)
    state = lax.while_loop(lambda s: s[0] < shortest, advance(range(rows)), state)
    for r in range(rows):
        state = lax.while_loop(lambda s, r=r: s[0] < ends[r], advance([r]), state)
    t, pool, total, arrive_up, arrive_down = state
    step = t[None]
    pool, _, _ = route(step, moves, pool, arrive_up, arrive_down)
    total = add_tiles(step, tasks, inverse_tiles, pool, total, cols)
    others = [swap(total[1, k], "row", rows, 1) for k in range(supers)]
    owner_row = row_owner.reshape(1, block_rows)
    inverse_rows, squares, owned = None, [], []
    for k in range(supers):
        earlier = [inverse_rows] + squares if k else []
        inverse_rows, *sums = finish(
            k, place, info, pole_order, pole_weights, owner_row, total, others[k],
            factor_block, diag_inverse, earlier, owners,
        )
        owned.append(sum_xor(sums[:owners], "pole", owners))
        squares = squares + sums[owners:]
    part = sum_xor(squares[supers - 1 :], "pole", owners)
    part = sum_xor([part] * rows, "row", rows)
    part = sum_xor([part] * cols, "col", cols)
    whole = [part] + [swap(part, "pole", owners, d) for d in range(1, owners)]
    block_density = arrange(place, whole).reshape(supers, width // supers, width // supers)
    owned = jnp.concatenate(owned, axis=1)
    return inverse_rows, owned[None], block_density


def product_high(left, right):
    return jnp.einsum("pts,psw->ptw", left, right, precision=lax.Precision.HIGHEST)


def contract(first, second):
    return jnp.einsum("pbks,pbkt->pkst", first, second, precision=lax.Precision.HIGHEST)


def shards(
    inverse_tiles,
    factor_block,
    diag_inverse,
    tile_pattern,
    ancestor_blocks,
    row_owner,
    pole_weights,
    pole_order,
):
    row_count = lax.axis_size("row")
    col_count = lax.axis_size("col")
    pole_total = lax.axis_size("pole")
    row_index = lax.axis_index("row")
    col_index = lax.axis_index("col")
    pole_index = lax.axis_index("pole")
    pole_count = inverse_tiles.shape[0]
    block_rows = inverse_tiles.shape[3]
    seg_cols = inverse_tiles.shape[4]
    width = factor_block.shape[3]
    supers = ancestor_blocks.shape[0]
    super_cols = width // supers
    own_block = row_index * col_count + col_index
    pattern_grid = tile_pattern.reshape(row_count, col_count, row_count, col_count).astype(
        jnp.float32
    )
    rows_pick = lax.dynamic_index_in_dim(pattern_grid, col_index, 1, keepdims=False)
    tiles_here = lax.dynamic_index_in_dim(rows_pick, row_index, 1, keepdims=False)
    col_keep = jnp.repeat(tiles_here, block_rows, axis=1)
    masked = inverse_tiles * col_keep[None, None, :, None, :]
    flattened = masked.reshape(pole_count, 2, row_count * block_rows, seg_cols)
    anc_keep = lax.dynamic_index_in_dim(ancestor_blocks, own_block, 1, keepdims=False).astype(
        jnp.float32
    )
    width_keep = jnp.repeat(anc_keep, super_cols)
    factor = factor_block * width_keep
    fac_piece = lax.all_gather(factor, "col", axis=2, tiled=True)
    real_part = product_high(flattened[:, 0], fac_piece[:, 0]) - product_high(
        flattened[:, 1], fac_piece[:, 1]
    )
    imag_part = product_high(flattened[:, 0], fac_piece[:, 1]) + product_high(
        flattened[:, 1], fac_piece[:, 0]
    )
    partial_value = jnp.stack([real_part, imag_part], axis=1)
    inverse_rows = (
        lax.psum_scatter(partial_value, "row", scatter_dimension=2, tiled=True) * width_keep
    )
    fac_split = factor.reshape(pole_count, 2, block_rows, supers, super_cols)
    rows_split = inverse_rows.reshape(pole_count, 2, block_rows, supers, super_cols)
    prod_real = contract(fac_split[:, 0], rows_split[:, 0]) - contract(
        fac_split[:, 1], rows_split[:, 1]
    )
    prod_imag = contract(fac_split[:, 0], rows_split[:, 1]) + contract(
        fac_split[:, 1], rows_split[:, 0]
    )
    order_here = lax.dynamic_slice_in_dim(pole_order, pole_index * pole_count, pole_count)
    table_hot = (
        order_here[:, None] == jnp.arange(pole_order.shape[0], dtype=jnp.int32)[None, :]
    ).astype(jnp.float32)
    weights = jnp.dot(
        table_hot, pole_weights, precision=lax.Precision.HIGHEST, preferred_element_type=jnp.float32
    )
    weight_real = weights[:, 0]
    weight_imag = weights[:, 1]
    summed_real, summed_imag = lax.psum((prod_real, prod_imag), ("row", "col"))
    green_real = diag_inverse[:, 0] - summed_real
    green_imag = diag_inverse[:, 1] - summed_imag
    local_kk = jnp.sum(
        weight_real[:, None, None, None] * green_imag
        + weight_imag[:, None, None, None] * green_real,
        axis=0,
    )
    block_density = lax.psum(local_kk, "pole")
    dens_local = jnp.sum(
        weight_real[:, None, None] * inverse_rows[:, 1]
        + weight_imag[:, None, None] * inverse_rows[:, 0],
        axis=0,
    )
    owner_ids = row_owner[:, 0]
    owner_hot = (owner_ids[:, None] == jnp.arange(pole_total, dtype=jnp.int32)[None, :]).astype(
        jnp.int32
    )
    owner_rank = jnp.cumsum(owner_hot, axis=0) - owner_hot
    rank_own = jnp.sum(owner_hot * owner_rank, axis=1)
    capacity = block_rows // 2
    slot_hit = (rank_own[:, None] == jnp.arange(capacity, dtype=jnp.int32)[None, :]).astype(
        jnp.float32
    )
    selector = jnp.transpose(
        owner_hot.astype(jnp.float32)[:, :, None] * slot_hit[:, None, :], (1, 2, 0)
    )
    summed_rows = lax.psum(dens_local, "pole")
    my_select = lax.dynamic_index_in_dim(selector, pole_index, 0, keepdims=True)
    owned_density = jnp.einsum(
        "pst,tw->psw", my_select, summed_rows, precision=lax.Precision.HIGHEST
    )
    return (inverse_rows, owned_density, block_density)


def solution(mesh):
    placed = (
        P("pole", None, None, "col", "row"),
        P("pole", None, ("row", "col"), None),
        P("pole", None, None, None, None),
        P(),
        P(),
        P(("row", "col"), None),
        P(),
        P(),
    )
    sizes = dict(mesh.shape)
    line_ok = sizes["row"] == 2 and sizes["col"] in (2, 4, 8) and sizes["pole"] in (2, 4, 8)

    def chosen(inverse_tiles, factor_block, *rest):
        tiled = factor_block.shape[2] % 256 == 0 and rest[2].shape[0] == 2
        run = sparse_shards if line_ok and tiled else shards
        return run(inverse_tiles, factor_block, *rest)

    return jax.shard_map(
        chosen,
        mesh=mesh,
        in_specs=placed,
        out_specs=(P("pole", None, ("row", "col"), None), P("pole", ("row", "col"), None), P()),
        check_vma=False,
    )
```

```python
import functools

import jax
import jax.numpy as jnp
from jax import lax
from jax.experimental import pallas as pl
from jax.experimental.pallas import tpu as pltpu
from jax.sharding import PartitionSpec as P

BF16 = jnp.bfloat16
VMEM_BYTES = 60 * 1024 * 1024


def smem():
    return pl.BlockSpec(memory_space=pltpu.SMEM)


def anywhere():
    return pl.BlockSpec(memory_space=pl.ANY)


def halves(value):
    high = value.astype(BF16)
    return high, (value - high.astype(jnp.float32)).astype(BF16)


def lowest_of(mask):
    return mask & -mask


def piece_index(bit, pieces):
    index = jnp.int32(-1)
    for i in range(pieces):
        index = jnp.where(bit == (1 << i), i, index)
    return index


def plan_kernel(
    rows, cols, supers, steps, place, pattern, keep, factor,
    info, moves, tasks, pool, arrive_up, arrive_down, total, stage, load_sems, store_sems,
):
    row, col = place[0], place[1]
    width = factor.shape[3] // supers
    pieces = supers * cols
    loads = [
        pltpu.make_async_copy(
            factor.at[:, :, :, pl.ds(k * width, width)], stage.at[k], load_sems.at[k]
        )
        for k in range(supers)
    ]
    stores = [
        pltpu.make_async_copy(stage.at[k], pool.at[k * cols + col], store_sems.at[k])
        for k in range(supers)
    ]
    for load in loads:
        load.start()
    for load, store in zip(loads, stores):
        load.wait()
        store.start()
    source = [sum(1 << i for i in range(c, pieces, cols)) for c in range(cols)]
    links = cols - 1

    def one_row(i, carry):
        r = lax.rem(row + 1 + i, rows)
        kept = jnp.int32(0)
        for k in range(supers):
            for c in range(cols):
                kept = kept | (keep[k, r * cols + c] << (k * cols + c))
        need = []
        for c2 in range(cols):
            mask = jnp.int32(0)
            for g in range(rows):
                bits = jnp.int32(0)
                for c in range(cols):
                    bits = bits | (pattern[g * cols + c2, r * cols + c] << c)
                for k in range(supers):
                    mask = mask | ((keep[k, g * cols + c2] * bits) << (k * cols))
            need.append(mask & kept & ~source[c2])
        up_need, down_need = [], []
        for l in range(links):
            above = functools.reduce(lambda a, b: a | b, need[l + 1 :])
            below = functools.reduce(lambda a, b: a | b, need[: l + 1])
            up_need.append(above & sum(source[: l + 1]))
            down_need.append(below & sum(source[l + 1 :]))

        def one_step(state):
            t, up_left, up_have, down_left, down_have = state
            up_bit, down_bit = [], []
            for l in range(links):
                ready = up_left[l] & up_have[l]
                pick = jnp.int32(0)
                for m in range(l, links):
                    part = ready & up_need[m]
                    pick = jnp.where(part != 0, part, pick)
                up_bit.append(lowest_of(pick))
                ready = down_left[l] & down_have[l + 1]
                pick = jnp.int32(0)
                for m in range(l, -1, -1):
                    part = ready & down_need[m]
                    pick = jnp.where(part != 0, part, pick)
                down_bit.append(lowest_of(pick))
            up_left = [left ^ bit for left, bit in zip(up_left, up_bit)]
            down_left = [left ^ bit for left, bit in zip(down_left, down_bit)]
            up_have = up_have[:1] + [have | bit for have, bit in zip(up_have[1:], up_bit)]
            down_have = [have | bit for have, bit in zip(down_have, down_bit)] + down_have[-1:]
            none = jnp.int32(0)
            send_up = sum([jnp.where(col == l, up_bit[l], none) for l in range(links)])
            send_down = sum([jnp.where(col == l + 1, down_bit[l], none) for l in range(links)])
            get_up = sum([jnp.where(col == l + 1, up_bit[l], none) for l in range(links)])
            get_down = sum([jnp.where(col == l, down_bit[l], none) for l in range(links)])
            for j, bit in enumerate((send_up, send_down, get_up, get_down)):
                moves[j, t] = piece_index(bit, pieces)
            return t + 1, up_left, up_have, down_left, down_have

        own = [jnp.int32(s) for s in source]

        def clear(t, done):
            for j in range(4):
                moves[j, t] = -1
            return done

        def unfinished(state):
            return functools.reduce(lambda a, b: a | b, state[1] + state[3]) != 0

        lax.fori_loop(0, steps + 1, clear, jnp.int32(0))
        state = (jnp.int32(0), up_need, own, down_need, own)
        info[r] = lax.while_loop(unfinished, one_step, state)[0]
        return carry

    lax.fori_loop(0, rows, one_row, jnp.int32(0))
    shortest, longest = info[row], info[row]
    for r in range(rows):
        shortest = jnp.minimum(shortest, info[r])
        longest = jnp.maximum(longest, info[r])
    ahead = jnp.int32(0)
    for r in range(rows):
        ahead = ahead | jnp.where(info[r] > info[row], 1, 0)
    early = jnp.where(shortest > 0, ahead, 0)
    info[rows + 2 * supers] = early

    def one_compute(s, touched):
        line = jnp.where((s == 0) & (early != 0), steps + 1, s)
        before = jnp.maximum(s - 1, 0)
        items = []
        for j in range(2):
            item = jnp.where(keep[j, row * cols + col] != 0, j * cols + col, -1)
            items.append(jnp.where(s == 0, item, moves[2 + j, before]))
        count = jnp.int32(0)
        previous = jnp.int32(-1)
        for j in range(1 + 2 * rows):
            tasks[line, j] = 0
        for g in range(rows):
            relative = lax.rem(g - row + rows, rows)
            for item in items:
                safe = jnp.maximum(item, 0)
                k = safe // cols
                c = safe - k * cols
                live = (
                    (item >= 0)
                    & (keep[k, g * cols + col] != 0)
                    & (pattern[g * cols + col, row * cols + c] != 0)
                )
                target = g * supers + k
                seen = (touched >> target) & 1
                joined = jnp.where(previous == target, 1, 0)
                code = (
                    safe + g * 256 + relative * 4096 + (1 - seen) * 65536 + joined * 131072
                )

                @pl.when(live)
                def _():
                    tasks[line, 1 + count] = code

                previous = jnp.where(live, target, previous)
                touched = jnp.where(live, touched | (1 << target), touched)
                count = jnp.where(live, count + 1, count)
        tasks[line, 0] = count
        return touched

    for j in range(1 + 2 * rows):
        tasks[0, j] = 0
        tasks[steps + 1, j] = 0
    touched = lax.fori_loop(0, longest + 1, one_compute, jnp.int32(0))
    for k in range(supers):
        info[rows + k] = (touched >> (row * supers + k)) & 1
        other = jnp.int32(0)
        partner = lax.rem(row + 1, rows)
        for c in range(cols):
            other = other | (
                keep[k, partner * cols + c] & pattern[row * cols + col, partner * cols + c]
            )
        info[rows + supers + k] = other & keep[k, row * cols + col]
        info[rows + 2 * supers + 1 + k] = (touched >> (partner * supers + k)) & 1
    for store in stores:
        store.wait()


def make_plan(place, pattern, keep, factor, rows, cols, steps):
    supers = keep.shape[0]
    poles, _, block_rows, width = factor.shape
    piece = (poles, 2, block_rows, width // supers)
    return pl.pallas_call(
        functools.partial(plan_kernel, rows, cols, supers, steps),
        out_shape=(
            jax.ShapeDtypeStruct((rows + 3 * supers + 1,), jnp.int32),
            jax.ShapeDtypeStruct((4, steps + 1), jnp.int32),
            jax.ShapeDtypeStruct((steps + 2, 1 + 2 * rows), jnp.int32),
            jax.ShapeDtypeStruct((supers * cols,) + piece, jnp.float32),
            jax.ShapeDtypeStruct(piece, jnp.float32),
            jax.ShapeDtypeStruct(piece, jnp.float32),
            jax.ShapeDtypeStruct((rows, supers) + piece, jnp.float32),
        ),
        in_specs=[smem(), smem(), smem(), anywhere()],
        out_specs=(smem(), smem(), smem(), anywhere(), anywhere(), anywhere(), anywhere()),
        scratch_shapes=[
            pltpu.VMEM((supers,) + piece, jnp.float32),
            pltpu.SemaphoreType.DMA((supers,)),
            pltpu.SemaphoreType.DMA((supers,)),
        ],
        compiler_params=pltpu.CompilerParams(vmem_limit_bytes=VMEM_BYTES),
        name="plan",
    )(place, pattern, keep, factor)


def route_kernel(
    step, moves, pool_in, arrive_up, arrive_down, pool, send_up, send_down,
    stage, load_sems, store_sems, send_sems,
):
    t = step[0]
    before = jnp.maximum(t - 1, 0)
    work = []
    for j, (arrived, leaving) in enumerate(((arrive_up, send_up), (arrive_down, send_down))):
        got = jnp.where(t > 0, moves[2 + j, before], -1)
        out = moves[j, t]
        fresh = (out >= 0) & (out == got)
        held = (out >= 0) & (out != got)
        load_held = pltpu.make_async_copy(
            pool.at[jnp.maximum(out, 0)], stage.at[2 + j], load_sems.at[2 + j]
        )
        load_got = pltpu.make_async_copy(arrived, stage.at[j], load_sems.at[j])
        send_held = pltpu.make_async_copy(stage.at[2 + j], leaving, send_sems.at[j])
        send_got = pltpu.make_async_copy(stage.at[j], leaving, send_sems.at[j])
        store = pltpu.make_async_copy(
            stage.at[j], pool.at[jnp.maximum(got, 0)], store_sems.at[j]
        )
        work.append((got >= 0, fresh, held, load_held, load_got, send_held, send_got, store))

    for _, _, held, load_held, _, _, _, _ in work:
        pl.when(held)(load_held.start)
    for come, _, _, _, load_got, _, _, _ in work:
        pl.when(come)(load_got.start)
    for _, _, held, load_held, _, send_held, _, _ in work:

        @pl.when(held)
        def _():
            load_held.wait()
            send_held.start()

    for come, fresh, _, _, load_got, _, send_got, store in work:

        @pl.when(come)
        def _():
            load_got.wait()
            pl.when(fresh)(send_got.start)
            store.start()

    for come, fresh, held, _, _, send_held, send_got, store in work:
        pl.when(held)(send_held.wait)
        pl.when(fresh)(send_got.wait)
        pl.when(come)(store.wait)


def route(step, moves, pool, arrive_up, arrive_down):
    piece = jax.ShapeDtypeStruct(arrive_up.shape, jnp.float32)
    return pl.pallas_call(
        route_kernel,
        out_shape=(jax.ShapeDtypeStruct(pool.shape, jnp.float32), piece, piece),
        in_specs=[smem(), smem(), anywhere(), anywhere(), anywhere()],
        out_specs=(anywhere(), anywhere(), anywhere()),
        input_output_aliases={2: 0},
        scratch_shapes=[
            pltpu.VMEM((4,) + arrive_up.shape, jnp.float32),
            pltpu.SemaphoreType.DMA((4,)),
            pltpu.SemaphoreType.DMA((2,)),
            pltpu.SemaphoreType.DMA((2,)),
        ],
        compiler_params=pltpu.CompilerParams(vmem_limit_bytes=VMEM_BYTES),
        name="route",
    )(step, moves, pool, arrive_up, arrive_down)


def tile_kernel(
    poles, step, tasks, tile, piece, total_in, total, left_hi, left_lo, right_hi, right_lo,
):
    position = pl.program_id(0)
    each = tasks[step[0], 0]
    count = each * poles
    spot = jnp.minimum(position, jnp.maximum(count - 1, 0))
    code = tasks[step[0], 1 + spot - lax.div(spot, jnp.maximum(each, 1)) * each]
    first = (code // 65536) % 2
    joined = code // 131072
    rows, depth = tile.shape[3], tile.shape[4]
    width = piece.shape[4]

    @pl.when((position == 0) & (count == 0))
    def _():
        total[...] = total_in[...]

    @pl.when(position < count)
    def _():
        @pl.when((joined == 0) & (first == 1))
        def _():
            total[...] = jnp.zeros_like(total)

        @pl.when((joined == 0) & (first == 0))
        def _():
            total[...] = total_in[...]

        for part in range(2):
            high, low = halves(tile[0, part, 0])
            left_hi[:, part * depth : (part + 1) * depth] = high
            left_lo[:, part * depth : (part + 1) * depth] = low
            high, low = halves(piece[0, 0, part])
            here = slice(part * depth, (part + 1) * depth)
            there = slice((1 - part) * depth, (2 - part) * depth)
            right_hi[here, :width] = high if part == 0 else -high
            right_lo[here, :width] = low if part == 0 else -low
            right_hi[there, width:] = high
            right_lo[there, width:] = low
        chunk = min(256, rows)
        for start in range(0, rows, chunk):
            span = slice(start, start + chunk)
            value = jnp.dot(
                left_hi[span, :], right_hi[...], preferred_element_type=jnp.float32
            )
            value += jnp.dot(
                left_hi[span, :], right_lo[...], preferred_element_type=jnp.float32
            )
            value += jnp.dot(
                left_lo[span, :], right_hi[...], preferred_element_type=jnp.float32
            )
            total[0, 0, 0, 0, span, :] += value[:, :width]
            total[0, 0, 0, 1, span, :] += value[:, width:]


def add_tiles(step, tasks, tiles, pool, total, cols):
    poles, block_rows, piece_cols = total.shape[2], *total.shape[4:]
    slots = tasks.shape[1] - 1

    def task_of(i, step, tasks):
        each = tasks[step[0], 0]
        spot = jnp.minimum(i, jnp.maximum(each * poles - 1, 0))
        q = lax.div(spot, jnp.maximum(each, 1))
        return q, tasks[step[0], 1 + spot - q * each]

    def tile_at(i, step, tasks):
        q, code = task_of(i, step, tasks)
        return q, 0, (code // 256) % 16, 0, (code % 256) % cols

    def piece_at(i, step, tasks):
        q, code = task_of(i, step, tasks)
        return code % 256, q, 0, 0, 0

    def total_at(i, step, tasks):
        q, code = task_of(i, step, tasks)
        return (code // 4096) % 16, (code % 256) // cols, q, 0, 0, 0

    total_spec = pl.BlockSpec((1, 1, 1, 2, block_rows, piece_cols), total_at)
    return pl.pallas_call(
        functools.partial(tile_kernel, poles),
        out_shape=jax.ShapeDtypeStruct(total.shape, jnp.float32),
        grid_spec=pltpu.PrefetchScalarGridSpec(
            num_scalar_prefetch=2,
            grid=(poles * slots,),
            in_specs=[
                pl.BlockSpec((1, 2, 1, block_rows, block_rows), tile_at),
                pl.BlockSpec((1, 1, 2, block_rows, piece_cols), piece_at),
                total_spec,
            ],
            out_specs=total_spec,
            scratch_shapes=[
                pltpu.VMEM((block_rows, 2 * block_rows), BF16),
                pltpu.VMEM((block_rows, 2 * block_rows), BF16),
                pltpu.VMEM((2 * block_rows, 2 * piece_cols), BF16),
                pltpu.VMEM((2 * block_rows, 2 * piece_cols), BF16),
            ],
        ),
        input_output_aliases={4: 0},
        compiler_params=pltpu.CompilerParams(
            dimension_semantics=("arbitrary",), vmem_limit_bytes=VMEM_BYTES
        ),
        cost_estimate=pl.CostEstimate(
            flops=poles * 6 * 8 * block_rows * block_rows * piece_cols,
            bytes_accessed=poles * 3 * 16 * block_rows * block_rows,
            transcendentals=0,
        ),
        name="tiles",
    )(step, tasks, tiles, pool, total)


def block_kernel(
    owners, place, info, order, table, partial, factor, sibling, diag, *rest,
):
    away, parts, block = rest
    rows, cols, supers = place[3], place[4], place[5]
    k, q, g = pl.program_id(0), pl.program_id(1), pl.program_id(2)
    poles = pl.num_programs(1)
    near = g == 0
    live = jnp.where(near, info[rows + k], info[rows + 2 * supers + 1 + k]) != 0
    pole = order[place[2] * poles + q]
    real, imag = table[pole, 0], table[pole, 1]

    @pl.when((q == 0) & near)
    def _():
        block[k] = jnp.zeros(block.shape[1:], jnp.float32)

    @pl.when(near & (place[0] * cols + place[1] == 0))
    def _():
        block[k] += real * diag[0, 1, 0] + imag * diag[0, 0, 0]

    def multiply(left_ref):
        y_real, y_imag = partial[0, 0, 0, 0], partial[0, 0, 0, 1]
        first = real * y_imag + imag * y_real
        second = real * y_real - imag * y_imag
        for left, right in ((left_ref[0, 0], first), (left_ref[0, 1], second)):
            left_hi, left_lo = halves(left)
            right_hi, right_lo = halves(right)
            for a, b in ((left_hi, right_hi), (left_hi, right_lo), (left_lo, right_hi)):
                block[k] -= lax.dot_general(
                    a, b, (((0,), (0,)), ((), ())), preferred_element_type=jnp.float32
                )

    @pl.when(live & near)
    def _():
        multiply(factor)

    @pl.when(live & jnp.logical_not(near))
    def _():
        multiply(sibling)

    @pl.when(jnp.logical_not(near))
    def _():
        away[...] = partial[0]

    final = (k == pl.num_programs(0) - 1) & (q == poles - 1) & (g == pl.num_programs(2) - 1)

    @pl.when(final)
    def _():
        height = parts.shape[1]
        share = block.shape[1] // height
        for d in range(owners):
            part = place[2] ^ d
            at = pl.multiple_of((part % share) * height, height)
            parts[d] = block[part // share, pl.ds(at, height), :]


def block_parts(place, info, order, table, total, factor, sibling, diag, owners):
    rows, supers, poles, _, block_rows, columns = total.shape
    parts = (owners, supers * columns // owners, columns)
    piece = pl.BlockSpec((1, 2, block_rows, columns), lambda k, q, g: (q, 0, 0, k))
    return pl.pallas_call(
        functools.partial(block_kernel, owners),
        out_shape=(jax.ShapeDtypeStruct(total.shape[1:], jnp.float32),)
        + (jax.ShapeDtypeStruct(parts, jnp.float32),),
        grid=(supers, poles, rows),
        in_specs=[smem(), smem(), smem(), smem()]
        + [
            pl.BlockSpec(
                (1, 1, 1, 2, block_rows, columns), lambda k, q, g: (g, k, q, 0, 0, 0)
            ),
            piece,
            piece,
            pl.BlockSpec((1, 2, 1, columns, columns), lambda k, q, g: (q, 0, k, 0, 0)),
        ],
        out_specs=(
            pl.BlockSpec((1, 1, 2, block_rows, columns), lambda k, q, g: (k, q, 0, 0, 0)),
        )
        + (pl.BlockSpec(parts, lambda k, q, g: (0, 0, 0)),),
        scratch_shapes=[pltpu.VMEM((supers, columns, columns), jnp.float32)],
        compiler_params=pltpu.CompilerParams(
            dimension_semantics=("arbitrary",) * 3, vmem_limit_bytes=VMEM_BYTES
        ),
        cost_estimate=pl.CostEstimate(
            flops=12 * rows * poles * supers * block_rows * columns * columns,
            bytes_accessed=4 * (total.size + 2 * factor.size),
            transcendentals=0,
        ),
        name="block",
    )(place, info, order, table, total, factor, sibling, diag)


def finish_kernel(
    owners, place, info, order, table, owner_row, own, other, after, result, *rest,
):
    packed, (dens, slot) = rest[:owners], rest[owners:]
    rows, supers = place[3], place[5]
    k, q = pl.program_id(0), pl.program_id(1)
    poles = pl.num_programs(1)
    height = own.shape[4]
    own_live = info[rows + k] != 0
    other_live = info[rows + supers + k] != 0
    pole = order[place[2] * poles + q]
    real, imag = table[pole, 0], table[pole, 1]

    @pl.when((k == 0) & (q == 0))
    def _():
        owner = owner_row[...]
        hot = lax.broadcasted_iota(jnp.int32, (8 * ((owners + 7) // 8), height), 0) == owner
        hot = hot.astype(jnp.float32)
        before = lax.broadcasted_iota(jnp.int32, (height, height), 0) < (
            lax.broadcasted_iota(jnp.int32, (height, height), 1)
        )
        ahead = jnp.dot(
            hot.astype(BF16), before.astype(jnp.float32).astype(BF16),
            preferred_element_type=jnp.float32,
        )
        slot[0:1, :] = jnp.sum(hot * ahead, axis=0, keepdims=True).astype(jnp.int32)
        slot[1:2, :] = owner ^ place[2]

    zero = jnp.zeros(own.shape[4:], jnp.float32)
    y_real = jnp.where(own_live, own[0, 0, 0, 0], zero)
    y_imag = jnp.where(own_live, own[0, 0, 0, 1], zero)
    y_real += jnp.where(other_live, other[0, 0, 0], zero)
    y_imag += jnp.where(other_live, other[0, 0, 1], zero)
    result[0, 0] = y_real
    result[0, 1] = y_imag
    term = real * y_imag + imag * y_real

    @pl.when(q == 0)
    def _():
        dens[...] = term

    @pl.when(q > 0)
    def _():
        dens[...] += term

    @pl.when(q == poles - 1)
    def _():
        high, low = halves(dens[...])
        for d in range(owners):
            capacity = packed[d].shape[0]
            mine = lax.broadcasted_iota(jnp.int32, (capacity, height), 0) == slot[0:1, :]
            mine = mine & (slot[1:2, :] == d)
            pick = mine.astype(jnp.float32).astype(BF16)
            packed[d][...] = jnp.dot(
                pick, high, preferred_element_type=jnp.float32
            ) + jnp.dot(pick, low, preferred_element_type=jnp.float32)


def finish(place, info, order, table, owner_row, total, other, after, owners):
    _, supers, poles, _, block_rows, columns = total.shape
    capacity = block_rows // 2
    return pl.pallas_call(
        functools.partial(finish_kernel, owners),
        out_shape=(
            jax.ShapeDtypeStruct((poles, 2, block_rows, supers * columns), jnp.float32),
        )
        + (jax.ShapeDtypeStruct((capacity, supers * columns), jnp.float32),) * owners,
        grid=(supers, poles),
        in_specs=[smem(), smem(), smem(), smem()]
        + [
            pl.BlockSpec((1, block_rows), lambda k, q: (0, 0)),
            pl.BlockSpec((1, 1, 1, 2, block_rows, columns), lambda k, q: (0, k, q, 0, 0, 0)),
            pl.BlockSpec((1, 1, 2, block_rows, columns), lambda k, q: (k, q, 0, 0, 0)),
            anywhere(),
        ],
        out_specs=(pl.BlockSpec((1, 2, block_rows, columns), lambda k, q: (q, 0, 0, k)),)
        + (pl.BlockSpec((capacity, columns), lambda k, q: (0, k)),) * owners,
        scratch_shapes=[
            pltpu.VMEM((block_rows, columns), jnp.float32),
            pltpu.VMEM((8, block_rows), jnp.int32),
        ],
        compiler_params=pltpu.CompilerParams(
            dimension_semantics=("arbitrary", "arbitrary"), vmem_limit_bytes=VMEM_BYTES
        ),
        cost_estimate=pl.CostEstimate(
            flops=8 * owners * capacity * block_rows * supers * columns,
            bytes_accessed=6 * total.size,
            transcendentals=0,
        ),
        name="finish",
    )(place, info, order, table, owner_row, total, other, after)


def swap(value, axis, size, distance):
    return lax.ppermute(value, axis, [(i, i ^ distance) for i in range(size)])


def sum_xor(values, axis, size):
    terms = [values[0]] + [swap(values[d], axis, size, d) for d in range(1, size)]
    return tree_sum(terms)


def tree_sum(terms):
    while len(terms) > 1:
        terms = [a + b for a, b in zip(terms[::2], terms[1::2])]
    return terms[0]


def add_kernel(mine, theirs, *outs):
    for d, out in enumerate(outs):
        out[...] = mine[d] + theirs[d]


def add_split(mine, theirs):
    return pl.pallas_call(
        add_kernel,
        out_shape=(jax.ShapeDtypeStruct(mine.shape[1:], jnp.float32),) * mine.shape[0],
        in_specs=[pl.BlockSpec(memory_space=pltpu.VMEM)] * 2,
        out_specs=(pl.BlockSpec(memory_space=pltpu.VMEM),) * mine.shape[0],
        name="add_split",
    )(mine, theirs)


def sum_kernel(after, *refs):
    refs[-1][...] = tree_sum([ref[...] for ref in refs[:-1]])


def add_after(after, terms):
    return pl.pallas_call(
        sum_kernel,
        out_shape=jax.ShapeDtypeStruct(terms[0].shape, jnp.float32),
        in_specs=[anywhere()] + [pl.BlockSpec(memory_space=pltpu.VMEM)] * len(terms),
        out_specs=pl.BlockSpec(memory_space=pltpu.VMEM),
        name="add_parts",
    )(after, *terms)


def arrange_kernel(place, *refs):
    parts, out = refs[:-1], refs[-1]
    height = parts[0].shape[0]
    for d, part in enumerate(parts):
        start = pl.multiple_of((place[2] ^ d) * height, height)
        out[pl.ds(start, height), :] = part[...]


def arrange(place, parts):
    height, width = parts[0].shape
    return pl.pallas_call(
        arrange_kernel,
        out_shape=jax.ShapeDtypeStruct((height * len(parts), width), jnp.float32),
        in_specs=[smem()] + [pl.BlockSpec(memory_space=pltpu.VMEM)] * len(parts),
        out_specs=pl.BlockSpec(memory_space=pltpu.VMEM),
        name="arrange",
    )(place, *parts)


def sparse_shards(
    inverse_tiles, factor_block, diag_inverse, tile_pattern, ancestor_blocks, row_owner,
    pole_weights, pole_order,
):
    rows = lax.axis_size("row")
    cols = lax.axis_size("col")
    owners = lax.axis_size("pole")
    supers = ancestor_blocks.shape[0]
    block_rows, width = factor_block.shape[2:]
    steps = supers * cols * (cols - 1) // 2
    place = jnp.stack(
        [
            lax.axis_index("row"), lax.axis_index("col"), lax.axis_index("pole"),
            jnp.int32(rows), jnp.int32(cols), jnp.int32(supers),
        ]
    ).astype(jnp.int32)
    sibling = swap(factor_block, "row", rows, 1)
    info, moves, tasks, pool, arrive_up, arrive_down, total = make_plan(
        place, tile_pattern, ancestor_blocks, factor_block, rows, cols, steps
    )
    ends = [info[r] for r in range(rows)]

    def advance(members):
        up = [(r * cols + c, r * cols + c + 1) for r in members for c in range(cols - 1)]
        down = [(b, a) for a, b in up]

        def body(state):
            t, pool, total, arrive_up, arrive_down = state
            step = t[None]
            pool, send_up, send_down = route(step, moves, pool, arrive_up, arrive_down)
            arrive_up = lax.ppermute(send_up, ("row", "col"), up)
            arrive_down = lax.ppermute(send_down, ("row", "col"), down)
            total = add_tiles(step, tasks, inverse_tiles, pool, total, cols)
            return t + 1, pool, total, arrive_up, arrive_down

        return body

    total = lax.cond(
        info[rows + 2 * supers] != 0,
        lambda held: add_tiles(
            jnp.full((1,), steps + 1, jnp.int32), tasks, inverse_tiles, pool, held, cols
        ),
        lambda held: held,
        total,
    )
    state = (jnp.int32(0), pool, total, arrive_up, arrive_down)
    shortest = functools.reduce(jnp.minimum, ends)
    state = lax.while_loop(lambda s: s[0] < shortest, advance(range(rows)), state)
    for r in range(rows):
        state = lax.while_loop(lambda s, r=r: s[0] < ends[r], advance([r]), state)
    t, pool, total, arrive_up, arrive_down = state
    step = t[None]
    pool, _, _ = route(step, moves, pool, arrive_up, arrive_down)
    total = add_tiles(step, tasks, inverse_tiles, pool, total, cols)
    away, parts = block_parts(
        place, info, pole_order, pole_weights, total, factor_block, sibling, diag_inverse, owners
    )
    other = swap(away, "row", rows, 1)
    inverse_rows, *packed = finish(
        place, info, pole_order, pole_weights, row_owner.reshape(1, block_rows), total, other,
        parts, owners,
    )
    split = add_split(parts, swap(parts, "row", rows, 1))
    terms = [split[0]] + [swap(split[d], "pole", owners, d) for d in range(1, owners)]
    part = add_after(packed[0], terms)
    part = sum_xor([part] * cols, "col", cols)
    whole = [part] + [swap(part, "pole", owners, d) for d in range(1, owners)]
    block_density = arrange(place, whole).reshape(supers, width // supers, width // supers)
    owned = sum_xor(packed, "pole", owners)
    return inverse_rows, owned[None], block_density


def product_high(left, right):
    return jnp.einsum("pts,psw->ptw", left, right, precision=lax.Precision.HIGHEST)


def contract(first, second):
    return jnp.einsum("pbks,pbkt->pkst", first, second, precision=lax.Precision.HIGHEST)


def shards(
    inverse_tiles,
    factor_block,
    diag_inverse,
    tile_pattern,
    ancestor_blocks,
    row_owner,
    pole_weights,
    pole_order,
):
    row_count = lax.axis_size("row")
    col_count = lax.axis_size("col")
    pole_total = lax.axis_size("pole")
    row_index = lax.axis_index("row")
    col_index = lax.axis_index("col")
    pole_index = lax.axis_index("pole")
    pole_count = inverse_tiles.shape[0]
    block_rows = inverse_tiles.shape[3]
    seg_cols = inverse_tiles.shape[4]
    width = factor_block.shape[3]
    supers = ancestor_blocks.shape[0]
    super_cols = width // supers
    own_block = row_index * col_count + col_index
    pattern_grid = tile_pattern.reshape(row_count, col_count, row_count, col_count).astype(
        jnp.float32
    )
    rows_pick = lax.dynamic_index_in_dim(pattern_grid, col_index, 1, keepdims=False)
    tiles_here = lax.dynamic_index_in_dim(rows_pick, row_index, 1, keepdims=False)
    col_keep = jnp.repeat(tiles_here, block_rows, axis=1)
    masked = inverse_tiles * col_keep[None, None, :, None, :]
    flattened = masked.reshape(pole_count, 2, row_count * block_rows, seg_cols)
    anc_keep = lax.dynamic_index_in_dim(ancestor_blocks, own_block, 1, keepdims=False).astype(
        jnp.float32
    )
    width_keep = jnp.repeat(anc_keep, super_cols)
    factor = factor_block * width_keep
    fac_piece = lax.all_gather(factor, "col", axis=2, tiled=True)
    real_part = product_high(flattened[:, 0], fac_piece[:, 0]) - product_high(
        flattened[:, 1], fac_piece[:, 1]
    )
    imag_part = product_high(flattened[:, 0], fac_piece[:, 1]) + product_high(
        flattened[:, 1], fac_piece[:, 0]
    )
    partial_value = jnp.stack([real_part, imag_part], axis=1)
    inverse_rows = (
        lax.psum_scatter(partial_value, "row", scatter_dimension=2, tiled=True) * width_keep
    )
    fac_split = factor.reshape(pole_count, 2, block_rows, supers, super_cols)
    rows_split = inverse_rows.reshape(pole_count, 2, block_rows, supers, super_cols)
    prod_real = contract(fac_split[:, 0], rows_split[:, 0]) - contract(
        fac_split[:, 1], rows_split[:, 1]
    )
    prod_imag = contract(fac_split[:, 0], rows_split[:, 1]) + contract(
        fac_split[:, 1], rows_split[:, 0]
    )
    order_here = lax.dynamic_slice_in_dim(pole_order, pole_index * pole_count, pole_count)
    table_hot = (
        order_here[:, None] == jnp.arange(pole_order.shape[0], dtype=jnp.int32)[None, :]
    ).astype(jnp.float32)
    weights = jnp.dot(
        table_hot, pole_weights, precision=lax.Precision.HIGHEST, preferred_element_type=jnp.float32
    )
    weight_real = weights[:, 0]
    weight_imag = weights[:, 1]
    summed_real, summed_imag = lax.psum((prod_real, prod_imag), ("row", "col"))
    green_real = diag_inverse[:, 0] - summed_real
    green_imag = diag_inverse[:, 1] - summed_imag
    local_kk = jnp.sum(
        weight_real[:, None, None, None] * green_imag
        + weight_imag[:, None, None, None] * green_real,
        axis=0,
    )
    block_density = lax.psum(local_kk, "pole")
    dens_local = jnp.sum(
        weight_real[:, None, None] * inverse_rows[:, 1]
        + weight_imag[:, None, None] * inverse_rows[:, 0],
        axis=0,
    )
    owner_ids = row_owner[:, 0]
    owner_hot = (owner_ids[:, None] == jnp.arange(pole_total, dtype=jnp.int32)[None, :]).astype(
        jnp.int32
    )
    owner_rank = jnp.cumsum(owner_hot, axis=0) - owner_hot
    rank_own = jnp.sum(owner_hot * owner_rank, axis=1)
    capacity = block_rows // 2
    slot_hit = (rank_own[:, None] == jnp.arange(capacity, dtype=jnp.int32)[None, :]).astype(
        jnp.float32
    )
    selector = jnp.transpose(
        owner_hot.astype(jnp.float32)[:, :, None] * slot_hit[:, None, :], (1, 2, 0)
    )
    summed_rows = lax.psum(dens_local, "pole")
    my_select = lax.dynamic_index_in_dim(selector, pole_index, 0, keepdims=True)
    owned_density = jnp.einsum(
        "pst,tw->psw", my_select, summed_rows, precision=lax.Precision.HIGHEST
    )
    return (inverse_rows, owned_density, block_density)


def solution(mesh):
    placed = (
        P("pole", None, None, "col", "row"),
        P("pole", None, ("row", "col"), None),
        P("pole", None, None, None, None),
        P(),
        P(),
        P(("row", "col"), None),
        P(),
        P(),
    )
    sizes = dict(mesh.shape)
    line_ok = sizes["row"] == 2 and sizes["col"] in (2, 4, 8) and sizes["pole"] in (2, 4, 8)

    def chosen(inverse_tiles, factor_block, *rest):
        tiled = factor_block.shape[2] % 256 == 0 and rest[2].shape[0] == 2
        run = sparse_shards if line_ok and tiled else shards
        return run(inverse_tiles, factor_block, *rest)

    return jax.shard_map(
        chosen,
        mesh=mesh,
        in_specs=placed,
        out_specs=(P("pole", None, ("row", "col"), None), P("pole", ("row", "col"), None), P()),
        check_vma=False,
    )
```
